128 devices in a mesh: cx: 16 (over y_lo, x, core), cy: 8 (over y_hi, z).
Axes of the slice: x: 4, y: 4 (y_hi: 2, y_lo: 2; y = y_hi * 2 + y_lo), z: 4, core: 2. Of those that a mesh axis runs over, the one named last changes fastest.
Arguments:
- signal: float32 [16384, 1024], P(('cx', 'cy')), may hold values from -6 to 6
- fan_cut: int32 [16384], replicated, may hold values from 0 to 255
Outputs:
- correlation: float32 [16384, 4096], P(('cx', 'cy'))
The draws below stay inside these ranges and needn't reach their ends.
All inputs are finite; a program needn't handle non-finite values.
Results may differ from the reference program's by a relative error of at most 0.0032.
Values may be sent and summed in bfloat16 or wider, within the bound.
A program may use at most 64 MiB of HBM per device.

```python
import math
import jax
import jax.numpy as jnp
from jax import lax

CH_DEV = 128
NT = 1024
BAND = 256
LAGS = 16
CHANNELS = 16384


def set_ends(array, rng, least, high):
    longest = array.shape.index(max(array.shape))
    spots = []
    for shift in (0, 1):
        where = [jax.random.randint(jax.random.fold_in(rng, axis), (), 0, length) for axis, length in enumerate(array.shape)]
        where[longest] = (where[longest] + shift) % array.shape[longest]
        spots.append(tuple(where))
    return array.at[spots[0]].set(least).at[spots[1]].set(high)


def levels(rng, dims, shards, low, top_value):
    level = 1.0
    for axis_at, shards_of in shards:
        steps = jax.random.uniform(jax.random.fold_in(jax.random.fold_in(rng, 6), axis_at), (shards_of,), jnp.float32, low / len(shards), top_value / len(shards))
        level = level * jnp.repeat(jnp.exp(steps), dims[axis_at] // shards_of).reshape((-1,) + (1,) * (len(dims) - 1 - axis_at))
    return level


def centred(stream_key, dims, deviation, reach, split=(), kind=jnp.bfloat16):
    array = jax.random.normal(stream_key, dims, jnp.float32) * deviation
    if len(split) > 0:
        array = levels(stream_key, dims, split, -0.22, 0.18) * array
    return jnp.clip(array, min=-reach, max=reach).astype(kind)


def setup_inputs(seed: int = 0) -> dict:
    streams_of = jax.random.split(jax.random.key(seed), 3)
    signal = centred(streams_of[0], (CHANNELS, NT), 1.0, 6.0, ((0, 128),), jnp.float32)
    fan_cut = set_ends(jax.random.randint(streams_of[1], (CHANNELS,), 0, NT // 4), jax.random.fold_in(streams_of[1], 1), 0, (NT // 4) - 1).astype(jnp.int32)
    return {"signal": signal, "fan_cut": fan_cut}


def block_correlate(own_rows, extended):
    count_rows = own_rows.shape[0]
    ext_rows = extended.shape[0]
    shifted = jnp.stack([jnp.pad(own_rows, ((0, 0), (offset, 0)))[:, :NT] for offset in range(LAGS)])
    products = jnp.einsum('lrt,mt->lrm', shifted.astype(jnp.float32), extended.astype(jnp.float32), precision=lax.Precision.HIGHEST)
    flattened = jnp.pad(products.reshape(LAGS, count_rows * ext_rows), ((0, 0), (0, count_rows)))
    banded = flattened.reshape(LAGS, count_rows, ext_rows + 1)[:, :, :BAND]
    return banded.transpose(1, 2, 0).reshape(count_rows, BAND * LAGS) * (1.0 / math.sqrt(NT))

def reference(signal, fan_cut):
    spectrum = jnp.fft.fft2(signal)
    freq_index = jnp.arange(NT, dtype=jnp.int32)
    freq_bin = jnp.minimum(freq_index, NT - freq_index)
    thresh = jnp.maximum(fan_cut, jnp.roll(fan_cut[::-1], 1))
    passband = freq_bin[None, :] >= thresh[:, None]
    filtered = jnp.real(jnp.fft.ifft2(jnp.where(passband, spectrum, 0.0)))
    filtered_bf = filtered.astype(jnp.bfloat16)
    half_band = BAND // 2
    padded = jnp.pad(filtered_bf, ((half_band, half_band), (0, 0)))

    def one_block(block_index):
        start_row = block_index * CH_DEV
        own_rows = lax.dynamic_slice_in_dim(filtered_bf, start_row, CH_DEV, 0)
        extended = lax.dynamic_slice_in_dim(padded, start_row, CH_DEV + BAND, 0)
        return block_correlate(own_rows, extended)
    results = lax.map(one_block, jnp.arange(CHANNELS // CH_DEV, dtype=jnp.int32))
    return results.reshape(CHANNELS, BAND * LAGS)
```

```python
import functools
import math

import jax
import jax.numpy as jnp
import numpy as np
from jax import lax
from jax.experimental import pallas as pl
from jax.experimental.pallas import tpu as pltpu
from jax.sharding import PartitionSpec as P

BAND = 256
LAGS = 16
BINS = 256
OWN = 128
LENGTH = 1024
MESH = pl.DeviceIdType.MESH
F32 = jnp.float32
BF16 = jnp.bfloat16


def halves(table):
    high = table.astype(BF16)
    return high, (table - high.astype(np.float64)).astype(BF16)


def tables(groups):
    bin_index = np.arange(BINS, dtype=np.int64)
    angle = 2.0 * math.pi / LENGTH * (bin_index[:, None] * np.arange(LENGTH)[None, :] % LENGTH)
    pairs = np.stack([np.cos(angle), -np.sin(angle)], axis=1).reshape(groups, 2, 2, LENGTH)
    time = pairs.transpose(0, 2, 1, 3).reshape(2 * BINS, LENGTH)
    index = np.arange(groups)
    angle = 2.0 * math.pi / groups * (index[:, None] * index[None, :] % groups)
    re, im = np.cos(angle), -np.sin(angle)
    wide = np.block([[re, -im], [im, re]])
    angle = 2.0 * math.pi / (groups * OWN) * (index[:, None] * index[None, :])
    twist = np.stack([np.cos(angle), np.sin(angle)]).astype(np.float32)
    return (*halves(time), *halves(wide), *halves(wide.T), twist)


def dot(left, right, dims=((1,), (0,))):
    return lax.dot_general(left, right, (dims, ((), ())), preferred_element_type=F32)


def split(value):
    high = value.astype(BF16)
    return high, (value - high.astype(F32)).astype(BF16)


def dot_three(left, right):
    return dot(left[0], right[0]) + (dot(left[0], right[1]) + dot(left[1], right[0]))


def blocks(value):
    return value[:OWN, :OWN], value[:OWN, OWN:], value[OWN:, :OWN], value[OWN:, OWN:]


def join(a, b, c, d):
    return jnp.concatenate([jnp.concatenate([a, b], axis=1), jnp.concatenate([c, d], axis=1)], axis=0)


def least_cut(cut):
    row = lax.broadcasted_iota(jnp.int32, (OWN, OWN), 0)
    col = lax.broadcasted_iota(jnp.int32, (OWN, OWN), 1)
    mirror = (((row + col) % OWN) == 0).astype(F32).astype(BF16)
    reverse = ((row + col) == OWN - 1).astype(F32).astype(BF16)
    exact = cut.astype(F32).astype(BF16)
    across = dot(exact, mirror).astype(BF16)
    mirrored = jnp.where(col == 0, dot(mirror, across), dot(reverse, across))
    return jnp.maximum(cut.astype(F32), mirrored).T


def filter_kernel(
    groups, inner,
    signal, cut, time_high, time_low, wide_high, wide_low, flip_high, flip_low, twist,
    ext,
    out_first, in_first, out_second, in_second,
    send_first, recv_first, send_second, recv_second, send_halo, recv_halo,
):
    me = lax.axis_index("cx") * inner + lax.axis_index("cy")

    def at(device):
        return (device // inner, device % inner)

    def peer(step):
        return lax.rem(me + step, groups)

    barrier = pltpu.get_barrier_semaphore()

    def greet(step, carry):
        pl.semaphore_signal(barrier, inc=1, device_id=at(peer(step)), device_id_type=MESH)
        return carry

    lax.fori_loop(1, groups, greet, 0)

    own_high, own_low = split(signal[...])
    both = jnp.concatenate([own_high, own_low], axis=0)
    wide_sum = dot(time_high[...], both, ((1,), (1,)))
    spectrum = (wide_sum[:, :OWN] + wide_sum[:, OWN:]) + dot(time_low[...], own_high, ((1,), (1,)))
    out_first[...] = spectrum.reshape(groups, 4, OWN)

    pl.semaphore_wait(barrier, groups - 1)

    def exchange(outgoing, incoming, send_sem, recv_sem):
        def push(step, carry):
            target = peer(step)
            pltpu.make_async_remote_copy(
                src_ref=outgoing.at[target],
                dst_ref=incoming.at[me],
                send_sem=send_sem,
                recv_sem=recv_sem,
                device_id=at(target),
                device_id_type=MESH,
            ).start()
            return carry

        lax.fori_loop(1, groups, push, 0)
        incoming[me] = outgoing[me]

    def settle(outgoing, incoming, send_sem, recv_sem):
        rest = pltpu.make_async_remote_copy(
            src_ref=outgoing.at[pl.ds(0, groups - 1)],
            dst_ref=incoming.at[pl.ds(0, groups - 1)],
            send_sem=send_sem,
            recv_sem=recv_sem,
            device_id=at(peer(1)),
            device_id_type=MESH,
        )
        rest.wait()

    exchange(out_first, in_first, send_first, recv_first)
    cut_least = least_cut(cut[...])
    wide = (wide_high[...], wide_low[...])
    flip = (flip_high[...], flip_low[...])
    cosine, sine = twist[0], twist[1]
    settle(out_first, in_first, send_first, recv_first)

    rows = [in_first[:, part, :] for part in range(4)]
    value = dot_three(wide, split(join(*rows)))
    re_a, re_b, im_a, im_b = blocks(value)
    value = join(
        re_a * cosine + im_a * sine, im_a * cosine - re_a * sine,
        re_b * cosine + im_b * sine, im_b * cosine - re_b * sine,
    )
    value = dot_three(split(value), flip)
    even = (2 * me).astype(F32)
    scale = -2.0 / (LENGTH * groups * OWN)
    keep_a = jnp.where(cut_least > even, jnp.where(me == 0, 0.5 * scale, scale), 0.0)
    keep_b = jnp.where(cut_least > even + 1.0, scale, 0.0)
    value = value * join(keep_a, keep_a, keep_b, keep_b)
    value = dot_three(split(value), wide)
    re_a, im_a, re_b, im_b = blocks(value)
    value = join(
        re_a * cosine - im_a * sine, re_b * cosine - im_b * sine,
        im_a * cosine + re_a * sine, im_b * cosine + re_b * sine,
    )
    value = dot_three(flip, split(value))
    for part, block in enumerate(blocks(value)):
        out_second[:, part, :] = block

    exchange(out_second, in_second, send_second, recv_second)
    settle(out_second, in_second, send_second, recv_second)

    back_high, back_low = split(in_second[...].reshape(4 * groups, OWN).T)
    both = jnp.concatenate([back_high, back_low], axis=0)
    halos = []
    chunk = 256
    for number in range(LENGTH // chunk):
        span = pl.ds(number * chunk, chunk)
        high, low = time_high[:, span], time_low[:, span]
        sums = dot(both, high)
        rejected = (sums[:OWN] + sums[OWN:]) + dot(back_high, low)
        ext[pl.ds(OWN, OWN), span] = (signal[:, span] + rejected).astype(BF16)
        source = ext.at[pl.ds(OWN, OWN), span]
        halos.append((
            pltpu.make_async_remote_copy(
                src_ref=source, dst_ref=ext.at[pl.ds(0, OWN), span],
                send_sem=send_halo.at[0, number], recv_sem=recv_halo.at[0, number],
                device_id=at(peer(1)), device_id_type=MESH,
            ),
            pltpu.make_async_remote_copy(
                src_ref=source, dst_ref=ext.at[pl.ds(2 * OWN, OWN), span],
                send_sem=send_halo.at[1, number], recv_sem=recv_halo.at[1, number],
                device_id=at(peer(groups - 1)), device_id_type=MESH,
            ),
        ))
        for copy in halos[-1]:
            copy.start()
    for pair in halos:
        for copy in pair:
            copy.wait()

    @pl.when(me == 0)
    def _():
        ext[pl.ds(0, OWN), :] = jnp.zeros((OWN, LENGTH), BF16)

    @pl.when(me == groups - 1)
    def _():
        ext[pl.ds(2 * OWN, OWN), :] = jnp.zeros((OWN, LENGTH), BF16)


def correlate_kernel(ext, out, lagged):
    own = ext[pl.ds(OWN, OWN), :] * jnp.asarray(1.0 / math.sqrt(LENGTH), BF16)

    def shifted(lag):
        if lag == 0:
            return own
        return jnp.concatenate([jnp.zeros((OWN, lag), BF16), own[:, :LENGTH - lag]], axis=1)

    everything = ext[...]
    count = ext.shape[0]
    for lag in range(0, LAGS, 2):
        pair = jnp.concatenate([shifted(lag), shifted(lag + 1)], axis=0)
        products = dot(everything, pair, ((1,), (1,)))
        lagged[pl.ds(lag, count, stride=LAGS), :] = products[:, :OWN]
        lagged[pl.ds(lag + 1, count, stride=LAGS), :] = products[:, OWN:]
    lane = lax.broadcasted_iota(jnp.int32, (8, OWN), 1)
    odd = [(lane // step) % 2 == 1 for step in (1, 2, 4)]
    tiles = BAND * LAGS // OWN
    for tile in range(tiles + OWN // 8 - 1):
        rows = [lagged[pl.ds(tile * OWN + 8 * number, 8), :] for number in range(OWN // 8 + 14)]
        for bit in range(3):
            gap = 2 << bit
            rows = [jnp.where(odd[bit], rows[at + gap], rows[at]) for at in range(len(rows) - gap)]
        turned = jnp.concatenate(rows, axis=0).T
        for group in range(max(0, tile - tiles + 1), min(OWN // 8, tile + 1)):
            out[pl.ds(8 * group, 8), (tile - group) * OWN:(tile - group + 1) * OWN] = turned[8 * group:8 * group + 8]


def body(groups, inner, signal, fan_cut):
    whole = pl.BlockSpec(memory_space=pltpu.VMEM)
    arrays = [jnp.asarray(table) for table in tables(groups)]
    message = pltpu.VMEM((groups, 4, OWN), F32)
    ext = pl.pallas_call(
        functools.partial(filter_kernel, groups, inner),
        out_shape=jax.ShapeDtypeStruct((3 * OWN, LENGTH), BF16),
        in_specs=[whole] * (2 + len(arrays)),
        out_specs=whole,
        scratch_shapes=[message] * 4 + [pltpu.SemaphoreType.DMA] * 4 + [pltpu.SemaphoreType.DMA((2, 4))] * 2,
        compiler_params=pltpu.CompilerParams(
            collective_id=0, has_side_effects=True, vmem_limit_bytes=40 * 2**20
        ),
        name="fan_filter",
    )(signal, fan_cut.reshape(OWN, groups), *arrays)
    return pl.pallas_call(
        correlate_kernel,
        out_shape=jax.ShapeDtypeStruct((OWN, BAND * LAGS), F32),
        in_specs=[whole],
        out_specs=whole,
        scratch_shapes=[pltpu.VMEM((3 * OWN * LAGS, OWN), F32)],
        compiler_params=pltpu.CompilerParams(vmem_limit_bytes=40 * 2**20),
        name="correlate",
    )(ext)


def solution(mesh):
    groups, inner = mesh.size, mesh.shape["cy"]
    return jax.shard_map(
        functools.partial(body, groups, inner),
        mesh=mesh,
        in_specs=(P(("cx", "cy"), None), P()),
        out_specs=P(("cx", "cy"), None),
        check_vma=False,
    )
```

```python
import functools
import math

import jax
import jax.numpy as jnp
import numpy as np
from jax import lax
from jax.experimental import pallas as pl
from jax.experimental.pallas import tpu as pltpu
from jax.sharding import PartitionSpec as P

BAND = 256
LAGS = 16
BINS = 256
OWN = 128
LENGTH = 1024
MESH = pl.DeviceIdType.MESH
F32 = jnp.float32
BF16 = jnp.bfloat16


def halves(table):
    high = table.astype(BF16)
    return high, (table - high.astype(np.float64)).astype(BF16)


def tables(groups):
    bin_index = np.arange(BINS, dtype=np.int64)
    angle = 2.0 * math.pi / LENGTH * (bin_index[:, None] * np.arange(LENGTH)[None, :] % LENGTH)
    pairs = np.stack([np.cos(angle), -np.sin(angle)], axis=1).reshape(groups, 2, 2, LENGTH)
    time = pairs.transpose(0, 2, 1, 3).reshape(2 * BINS, LENGTH)
    index = np.arange(groups)
    angle = 2.0 * math.pi / groups * (index[:, None] * index[None, :] % groups)
    re, im = np.cos(angle), -np.sin(angle)
    wide = np.block([[re, -im], [im, re]])
    angle = 2.0 * math.pi / (groups * OWN) * (index[:, None] * index[None, :])
    twist = np.stack([np.cos(angle), np.sin(angle)]).astype(np.float32)
    return np.stack(halves(time)), np.stack([*halves(wide), *halves(wide.T)]), twist


def dot(left, right, dims=((1,), (0,))):
    return lax.dot_general(left, right, (dims, ((), ())), preferred_element_type=F32)


def split(value):
    high = value.astype(BF16)
    return high, (value - high.astype(F32)).astype(BF16)


def dot_three(left, right):
    return dot(left[0], right[0]) + (dot(left[0], right[1]) + dot(left[1], right[0]))


def blocks(value):
    return value[:OWN, :OWN], value[:OWN, OWN:], value[OWN:, :OWN], value[OWN:, OWN:]


def join(a, b, c, d):
    return jnp.concatenate([jnp.concatenate([a, b], axis=1), jnp.concatenate([c, d], axis=1)], axis=0)


def least_cut(cut):
    row = lax.broadcasted_iota(jnp.int32, (OWN, OWN), 0)
    col = lax.broadcasted_iota(jnp.int32, (OWN, OWN), 1)
    mirror = (((row + col) % OWN) == 0).astype(F32).astype(BF16)
    reverse = ((row + col) == OWN - 1).astype(F32).astype(BF16)
    exact = cut.astype(F32).astype(BF16)
    across = dot(exact, mirror).astype(BF16)
    mirrored = jnp.where(col == 0, dot(mirror, across), dot(reverse, across))
    return jnp.maximum(cut.astype(F32), mirrored).T


def filter_kernel(
    groups, inner,
    signal_far, cut_far, time_far, wide_far, twist_far,
    out_far,
    signal, cut, time, wide_all, twist, load_sems,
    out_first, in_first, out_second, in_second,
    send_first, recv_first, send_second, recv_second, send_halo, recv_halo,
    ext, lags, partial, lagged, out, store_sem,
):
    outer_at, inner_at = lax.axis_index("cx"), lax.axis_index("cy")
    me = outer_at * inner + inner_at

    def at(device):
        return (device // inner, device % inner)

    def peer(step):
        return lax.rem(me + step, groups)

    def visit_others(visit):
        high, mid, core = outer_at // 8, lax.rem(outer_at // 2, 4), lax.rem(outer_at, 2)
        top, low = inner_at // 4, lax.rem(inner_at, 4)
        highs, cores, tops = [8 * high, 8 - 8 * high], [core, 1 - core], [4 * top, 4 - 4 * top]

        def near(mid_step, low_step, combinations):
            mid_to, low_to = 2 * lax.rem(mid + mid_step, 4), lax.rem(low + low_step, 4)
            for flip_top, flip_high, flip_core in combinations:
                visit(highs[flip_high] + mid_to + cores[flip_core], tops[flip_top] + low_to)

        every = [(i, j, k) for i in (1, 0) for j in (1, 0) for k in (1, 0)]

        def far(number):
            return number + 2 - (number // 2) * (2 * number - 1)

        def block(index, carry):
            near(far(index // 4), far(lax.rem(index, 4)), every)
            return carry

        lax.fori_loop(0, 15, block, 0)
        near(0, 0, every[:-1])

    pairs = ((signal_far, signal), (time_far.at[0], time.at[0]), (time_far.at[1], time.at[1]),
             (cut_far, cut), (wide_far, wide_all), (twist_far, twist))
    loads = [pltpu.make_async_copy(far, near, load_sems.at[number]) for number, (far, near) in enumerate(pairs)]
    for load in loads:
        load.start()

    barrier = pltpu.get_barrier_semaphore()

    def greet(cx, cy):
        pl.semaphore_signal(barrier, inc=1, device_id=(cx, cy), device_id_type=MESH)

    visit_others(greet)
    loads[0].wait()
    time_high, time_low = time.at[0], time.at[1]
    own_high, own_low = split(signal[...])
    both = jnp.concatenate([own_high, own_low], axis=0)
    loads[1].wait()
    wide_sum = dot(time_high[...], both, ((1,), (1,)))
    loads[2].wait()
    spectrum = (wide_sum[:, :OWN] + wide_sum[:, OWN:]) + dot(time_low[...], own_high, ((1,), (1,)))
    out_first[...] = spectrum.reshape(groups, 4, OWN)

    pl.semaphore_wait(barrier, groups - 1)

    def exchange(outgoing, incoming, send_sem, recv_sem):
        def push(cx, cy):
            pltpu.make_async_remote_copy(
                src_ref=outgoing.at[cx * inner + cy],
                dst_ref=incoming.at[me],
                send_sem=send_sem,
                recv_sem=recv_sem,
                device_id=(cx, cy),
                device_id_type=MESH,
            ).start()

        visit_others(push)
        incoming[me] = outgoing[me]

    def settle(outgoing, incoming, send_sem, recv_sem):
        rest = pltpu.make_async_remote_copy(
            src_ref=outgoing.at[pl.ds(0, groups - 1)],
            dst_ref=incoming.at[pl.ds(0, groups - 1)],
            send_sem=send_sem,
            recv_sem=recv_sem,
            device_id=at(peer(1)),
            device_id_type=MESH,
        )
        rest.wait()

    exchange(out_first, in_first, send_first, recv_first)
    for load in loads[3:]:
        load.wait()
    cut_least = least_cut(cut[...])
    wide = (wide_all[0], wide_all[1])
    flip = (wide_all[2], wide_all[3])
    cosine, sine = twist[0], twist[1]
    settle(out_first, in_first, send_first, recv_first)

    rows = [in_first[:, part, :] for part in range(4)]
    value = dot_three(wide, split(join(*rows)))
    re_a, re_b, im_a, im_b = blocks(value)
    value = join(
        re_a * cosine + im_a * sine, im_a * cosine - re_a * sine,
        re_b * cosine + im_b * sine, im_b * cosine - re_b * sine,
    )
    value = dot_three(split(value), flip)
    even = (2 * me).astype(F32)
    scale = -2.0 / (LENGTH * groups * OWN)
    keep_a = jnp.where(cut_least > even, jnp.where(me == 0, 0.5 * scale, scale), 0.0)
    keep_b = jnp.where(cut_least > even + 1.0, scale, 0.0)
    value = value * join(keep_a, keep_a, keep_b, keep_b)
    value = dot_three(split(value), wide)
    re_a, im_a, re_b, im_b = blocks(value)
    value = join(
        re_a * cosine - im_a * sine, re_b * cosine - im_b * sine,
        im_a * cosine + re_a * sine, im_b * cosine + re_b * sine,
    )
    value = dot_three(flip, split(value))
    for part, block in enumerate(blocks(value)):
        out_second[:, part, :] = block

    exchange(out_second, in_second, send_second, recv_second)
    settle(out_second, in_second, send_second, recv_second)

    back_high, back_low = split(in_second[...].reshape(4 * groups, OWN).T)
    both = jnp.concatenate([back_high, back_low], axis=0)
    halos = []
    chunk = 256
    for number in range(LENGTH // chunk):
        span = pl.ds(number * chunk, chunk)
        high, low = time_high[:, span], time_low[:, span]
        sums = dot(both, high)
        rejected = (sums[:OWN] + sums[OWN:]) + dot(back_high, low)
        ext[pl.ds(OWN, OWN), span] = (signal[:, span] + rejected).astype(BF16)
        source = ext.at[pl.ds(OWN, OWN), span]
        halos.append((
            pltpu.make_async_remote_copy(
                src_ref=source, dst_ref=ext.at[pl.ds(0, OWN), span],
                send_sem=send_halo.at[0, number], recv_sem=recv_halo.at[0, number],
                device_id=at(peer(1)), device_id_type=MESH,
            ),
            pltpu.make_async_remote_copy(
                src_ref=source, dst_ref=ext.at[pl.ds(2 * OWN, OWN), span],
                send_sem=send_halo.at[1, number], recv_sem=recv_halo.at[1, number],
                device_id=at(peer(groups - 1)), device_id_type=MESH,
            ),
        ))
        for copy in halos[-1]:
            copy.start()
    own = ext[pl.ds(OWN, OWN), :] * jnp.asarray(1.0 / math.sqrt(LENGTH), BF16)
    for lag in range(LAGS):
        lags[pl.ds(lag * OWN, OWN), :] = own if lag == 0 else jnp.concatenate(
            [jnp.zeros((OWN, lag), BF16), own[:, :LENGTH - lag]], axis=1
        )

    def products(rows, number, begin, length):
        return dot(rows, lags[pl.ds(number * 2 * OWN, 2 * OWN), begin:begin + length], ((1,), (1,)))

    def keep(block, number, values):
        for side in range(2):
            begin = block * OWN * LAGS + 2 * number + side
            lagged[pl.ds(begin, OWN, stride=LAGS), :] = values[:, side * OWN:(side + 1) * OWN]

    lane = lax.broadcasted_iota(jnp.int32, (8, OWN), 1)
    odd = [(lane // step) % 2 == 1 for step in (1, 2, 4)]
    tiles = BAND * LAGS // OWN
    tile_rows = OWN // 8

    def finish(first, last):
        for tile in range(first, last):
            rows = [lagged[pl.ds(tile * OWN + 8 * number, 8), :] for number in range(tile_rows + 14)]
            for bit in range(3):
                gap = 2 << bit
                rows = [jnp.where(odd[bit], rows[spot + gap], rows[spot]) for spot in range(len(rows) - gap)]
            turned = jnp.concatenate(rows, axis=0).T
            for group in range(max(0, tile - tiles + 1), min(tile_rows, tile + 1)):
                out[pl.ds(8 * group, 8), pl.ds((tile - group) * OWN, OWN)] = turned[8 * group:8 * group + 8]
        for group in range(tile_rows):
            begin, end = max(0, first - group), min(tiles, last - group)
            if begin < end:
                place = (pl.ds(8 * group, 8), pl.ds(begin * OWN, (end - begin) * OWN))
                pltpu.make_async_copy(out.at[place], out_far.at[place], store_sem).start()

    middle = ext[pl.ds(OWN, OWN), :]
    for number in range(LAGS // 2):
        keep(1, number, products(middle, number, 0, LENGTH))
    finish(tile_rows, 2 * tile_rows - 1)

    def arrive(numbers):
        for number in numbers:
            for copy in halos[number]:
                copy.wait_recv()
        span = pl.ds(numbers[0] * chunk, len(numbers) * chunk)

        @pl.when(me == 0)
        def _():
            ext[pl.ds(0, OWN), span] = jnp.zeros((OWN, len(numbers) * chunk), BF16)

        @pl.when(me == groups - 1)
        def _():
            ext[pl.ds(2 * OWN, OWN), span] = jnp.zeros((OWN, len(numbers) * chunk), BF16)

        return jnp.concatenate([ext[pl.ds(0, OWN), span], ext[pl.ds(2 * OWN, OWN), span]], axis=0)

    early = LENGTH - chunk
    sides = arrive(range(early // chunk))
    for number in range(LAGS // 2):
        partial[number] = products(sides, number, 0, early)
    sides = arrive([early // chunk])
    for number in range(LAGS // 2):
        total = partial[number] + products(sides, number, early, chunk)
        keep(0, number, total[:OWN])
        keep(2, number, total[OWN:])
    finish(0, tile_rows)
    finish(2 * tile_rows - 1, tiles + tile_rows - 1)
    for pair in halos:
        for copy in pair:
            copy.wait_send()
    pltpu.make_async_copy(out, out_far, store_sem).wait()


def body(groups, inner, signal, fan_cut):
    operands = [signal, fan_cut.reshape(OWN, groups), *(jnp.asarray(table) for table in tables(groups))]
    anywhere = pl.BlockSpec(memory_space=pl.ANY)
    message = pltpu.VMEM((groups, 4, OWN), F32)
    result = jax.ShapeDtypeStruct((OWN, BAND * LAGS), F32)
    return pl.pallas_call(
        functools.partial(filter_kernel, groups, inner),
        out_shape=result,
        in_specs=[anywhere] * len(operands),
        out_specs=anywhere,
        scratch_shapes=[pltpu.VMEM(array.shape, array.dtype) for array in operands]
        + [pltpu.SemaphoreType.DMA((len(operands) + 1,))]
        + [message] * 4 + [pltpu.SemaphoreType.DMA] * 4 + [pltpu.SemaphoreType.DMA((2, 4))] * 2
        + [
            pltpu.VMEM((3 * OWN, LENGTH), BF16),
            pltpu.VMEM((LAGS * OWN, LENGTH), BF16),
            pltpu.VMEM((LAGS // 2, 2 * OWN, 2 * OWN), F32),
            pltpu.VMEM((3 * OWN * LAGS, OWN), F32),
            pltpu.VMEM(result.shape, F32),
            pltpu.SemaphoreType.DMA,
        ],
        compiler_params=pltpu.CompilerParams(
            collective_id=0, has_side_effects=True, vmem_limit_bytes=56 * 2**20
        ),
        name="fan_filter_correlate",
    )(*operands)


def solution(mesh):
    groups, inner = mesh.size, mesh.shape["cy"]
    return jax.shard_map(
        functools.partial(body, groups, inner),
        mesh=mesh,
        in_specs=(P(("cx", "cy"), None), P()),
        out_specs=P(("cx", "cy"), None),
        check_vma=False,
    )
```

```python
import functools
import math

import jax
import jax.numpy as jnp
import numpy as np
from jax import lax
from jax.experimental import pallas as pl
from jax.experimental.pallas import tpu as pltpu
from jax.sharding import PartitionSpec as P

BAND = 256
LAGS = 16
BINS = 256
OWN = 128
LENGTH = 1024
MESH = pl.DeviceIdType.MESH
F32 = jnp.float32
BF16 = jnp.bfloat16


def halves(table):
    high = table.astype(BF16)
    return high, (table - high.astype(np.float64)).astype(BF16)


def tables(groups):
    bin_index = np.arange(BINS, dtype=np.int64)
    angle = 2.0 * math.pi / LENGTH * (bin_index[:, None] * np.arange(LENGTH)[None, :] % LENGTH)
    pairs = np.stack([np.cos(angle), -np.sin(angle)], axis=1).reshape(groups, 2, 2, LENGTH)
    time = pairs.transpose(0, 2, 1, 3).reshape(2 * BINS, LENGTH)
    index = np.arange(groups)
    angle = 2.0 * math.pi / groups * (index[:, None] * index[None, :] % groups)
    re, im = np.cos(angle), -np.sin(angle)
    wide = np.block([[re, -im], [im, re]])
    angle = 2.0 * math.pi / (groups * OWN) * (index[:, None] * index[None, :])
    twist = np.stack([np.cos(angle), np.sin(angle)]).astype(np.float32)
    return np.stack(halves(time)), np.stack([*halves(wide), *halves(wide.T)]), twist


def dot(left, right, dims=((1,), (0,))):
    return lax.dot_general(left, right, (dims, ((), ())), preferred_element_type=F32)


def split(value):
    high = value.astype(BF16)
    return high, (value - high.astype(F32)).astype(BF16)


def dot_three(left, right):
    return dot(left[0], right[0]) + (dot(left[0], right[1]) + dot(left[1], right[0]))


def blocks(value):
    return value[:OWN, :OWN], value[:OWN, OWN:], value[OWN:, :OWN], value[OWN:, OWN:]


def join(a, b, c, d):
    return jnp.concatenate([jnp.concatenate([a, b], axis=1), jnp.concatenate([c, d], axis=1)], axis=0)


def least_cut(cut):
    row = lax.broadcasted_iota(jnp.int32, (OWN, OWN), 0)
    col = lax.broadcasted_iota(jnp.int32, (OWN, OWN), 1)
    mirror = (((row + col) % OWN) == 0).astype(F32).astype(BF16)
    reverse = ((row + col) == OWN - 1).astype(F32).astype(BF16)
    exact = cut.astype(F32).astype(BF16)
    across = dot(exact, mirror).astype(BF16)
    mirrored = jnp.where(col == 0, dot(mirror, across), dot(reverse, across))
    return jnp.maximum(cut.astype(F32), mirrored).T


TILES = BAND * LAGS // OWN
TILE_ROWS = OWN // 8


def finish(lagged, out, first, last):
    lane = lax.broadcasted_iota(jnp.int32, (8, OWN), 1)
    odd = [(lane // step) % 2 == 1 for step in (1, 2, 4)]
    for tile in range(first, last):
        rows = [lagged[pl.ds(tile * OWN + 8 * number, 8), :] for number in range(TILE_ROWS + 14)]
        for bit in range(3):
            gap = 2 << bit
            rows = [jnp.where(odd[bit], rows[spot + gap], rows[spot]) for spot in range(len(rows) - gap)]
        turned = jnp.concatenate(rows, axis=0).T
        for group in range(max(0, tile - TILES + 1), min(TILE_ROWS, tile + 1)):
            out[pl.ds(8 * group, 8), pl.ds((tile - group) * OWN, OWN)] = turned[8 * group:8 * group + 8]


def filter_kernel(
    groups, inner,
    signal_far, cut_far, time_far, wide_far, twist_far,
    lagged, out,
    signal, cut, time, wide_all, twist, load_sems,
    out_first, in_first, out_second, in_second,
    send_first, recv_first, send_second, recv_second, send_halo, recv_halo,
    ext, lags, partial,
):
    outer_at, inner_at = lax.axis_index("cx"), lax.axis_index("cy")
    me = outer_at * inner + inner_at

    def at(device):
        return (device // inner, device % inner)

    def peer(step):
        return lax.rem(me + step, groups)

    def visit_others(visit):
        high, mid, core = outer_at // 8, lax.rem(outer_at // 2, 4), lax.rem(outer_at, 2)
        top, low = inner_at // 4, lax.rem(inner_at, 4)
        highs, cores, tops = [8 * high, 8 - 8 * high], [core, 1 - core], [4 * top, 4 - 4 * top]

        def near(mid_step, low_step, combinations):
            mid_to, low_to = 2 * lax.rem(mid + mid_step, 4), lax.rem(low + low_step, 4)
            for flip_top, flip_high, flip_core in combinations:
                visit(highs[flip_high] + mid_to + cores[flip_core], tops[flip_top] + low_to)

        every = [(i, j, k) for i in (1, 0) for j in (1, 0) for k in (1, 0)]

        def far(number):
            return number + 2 - (number // 2) * (2 * number - 1)

        def block(index, carry):
            near(far(index // 4), far(lax.rem(index, 4)), every)
            return carry

        lax.fori_loop(0, 15, block, 0)
        near(0, 0, every[:-1])

    pairs = ((signal_far, signal), (time_far.at[0], time.at[0]), (time_far.at[1], time.at[1]),
             (cut_far, cut), (wide_far, wide_all), (twist_far, twist))
    loads = [pltpu.make_async_copy(far, near, load_sems.at[number]) for number, (far, near) in enumerate(pairs)]
    for load in loads:
        load.start()

    barrier = pltpu.get_barrier_semaphore()

    def greet(cx, cy):
        pl.semaphore_signal(barrier, inc=1, device_id=(cx, cy), device_id_type=MESH)

    visit_others(greet)
    loads[0].wait()
    time_high, time_low = time.at[0], time.at[1]
    own_high, own_low = split(signal[...])
    both = jnp.concatenate([own_high, own_low], axis=0)
    loads[1].wait()
    wide_sum = dot(time_high[...], both, ((1,), (1,)))
    loads[2].wait()
    spectrum = (wide_sum[:, :OWN] + wide_sum[:, OWN:]) + dot(time_low[...], own_high, ((1,), (1,)))
    out_first[...] = spectrum.reshape(groups, 4, OWN)

    pl.semaphore_wait(barrier, groups - 1)

    def exchange(outgoing, incoming, send_sem, recv_sem):
        def push(cx, cy):
            pltpu.make_async_remote_copy(
                src_ref=outgoing.at[cx * inner + cy],
                dst_ref=incoming.at[me],
                send_sem=send_sem,
                recv_sem=recv_sem,
                device_id=(cx, cy),
                device_id_type=MESH,
            ).start()

        visit_others(push)
        incoming[me] = outgoing[me]

    def settle(outgoing, incoming, send_sem, recv_sem):
        rest = pltpu.make_async_remote_copy(
            src_ref=outgoing.at[pl.ds(0, groups - 1)],
            dst_ref=incoming.at[pl.ds(0, groups - 1)],
            send_sem=send_sem,
            recv_sem=recv_sem,
            device_id=at(peer(1)),
            device_id_type=MESH,
        )
        rest.wait()

    exchange(out_first, in_first, send_first, recv_first)
    for load in loads[3:]:
        load.wait()
    cut_least = least_cut(cut[...])
    wide = (wide_all[0], wide_all[1])
    flip = (wide_all[2], wide_all[3])
    cosine, sine = twist[0], twist[1]
    settle(out_first, in_first, send_first, recv_first)

    rows = [in_first[:, part, :] for part in range(4)]
    value = dot_three(wide, split(join(*rows)))
    re_a, re_b, im_a, im_b = blocks(value)
    value = join(
        re_a * cosine + im_a * sine, im_a * cosine - re_a * sine,
        re_b * cosine + im_b * sine, im_b * cosine - re_b * sine,
    )
    value = dot_three(split(value), flip)
    even = (2 * me).astype(F32)
    scale = -2.0 / (LENGTH * groups * OWN)
    keep_a = jnp.where(cut_least > even, jnp.where(me == 0, 0.5 * scale, scale), 0.0)
    keep_b = jnp.where(cut_least > even + 1.0, scale, 0.0)
    value = value * join(keep_a, keep_a, keep_b, keep_b)
    value = dot_three(split(value), wide)
    re_a, im_a, re_b, im_b = blocks(value)
    value = join(
        re_a * cosine - im_a * sine, re_b * cosine - im_b * sine,
        im_a * cosine + re_a * sine, im_b * cosine + re_b * sine,
    )
    value = dot_three(flip, split(value))
    for part, block in enumerate(blocks(value)):
        out_second[:, part, :] = block

    exchange(out_second, in_second, send_second, recv_second)
    settle(out_second, in_second, send_second, recv_second)

    back_high, back_low = split(in_second[...].reshape(4 * groups, OWN).T)
    both = jnp.concatenate([back_high, back_low], axis=0)
    halos = []
    chunk = 256
    for number in range(LENGTH // chunk):
        span = pl.ds(number * chunk, chunk)
        high, low = time_high[:, span], time_low[:, span]
        sums = dot(both, high)
        rejected = (sums[:OWN] + sums[OWN:]) + dot(back_high, low)
        ext[pl.ds(OWN, OWN), span] = (signal[:, span] + rejected).astype(BF16)
        source = ext.at[pl.ds(OWN, OWN), span]
        halos.append((
            pltpu.make_async_remote_copy(
                src_ref=source, dst_ref=ext.at[pl.ds(0, OWN), span],
                send_sem=send_halo.at[0, number], recv_sem=recv_halo.at[0, number],
                device_id=at(peer(1)), device_id_type=MESH,
            ),
            pltpu.make_async_remote_copy(
                src_ref=source, dst_ref=ext.at[pl.ds(2 * OWN, OWN), span],
                send_sem=send_halo.at[1, number], recv_sem=recv_halo.at[1, number],
                device_id=at(peer(groups - 1)), device_id_type=MESH,
            ),
        ))
        for copy in halos[-1]:
            copy.start()
    own = ext[pl.ds(OWN, OWN), :] * jnp.asarray(1.0 / math.sqrt(LENGTH), BF16)
    for lag in range(LAGS):
        lags[pl.ds(lag * OWN, OWN), :] = own if lag == 0 else jnp.concatenate(
            [jnp.zeros((OWN, lag), BF16), own[:, :LENGTH - lag]], axis=1
        )

    def products(rows, number, begin, length):
        return dot(rows, lags[pl.ds(number * 2 * OWN, 2 * OWN), begin:begin + length], ((1,), (1,)))

    def keep(block, number, values):
        for side in range(2):
            begin = block * OWN * LAGS + 2 * number + side
            lagged[pl.ds(begin, OWN, stride=LAGS), :] = values[:, side * OWN:(side + 1) * OWN]

    middle = ext[pl.ds(OWN, OWN), :]
    for number in range(LAGS // 2):
        keep(1, number, products(middle, number, 0, LENGTH))
    finish(lagged, out, TILE_ROWS, 2 * TILE_ROWS - 1)

    def arrive(numbers):
        for number in numbers:
            for copy in halos[number]:
                copy.wait_recv()
        span = pl.ds(numbers[0] * chunk, len(numbers) * chunk)

        @pl.when(me == 0)
        def _():
            ext[pl.ds(0, OWN), span] = jnp.zeros((OWN, len(numbers) * chunk), BF16)

        @pl.when(me == groups - 1)
        def _():
            ext[pl.ds(2 * OWN, OWN), span] = jnp.zeros((OWN, len(numbers) * chunk), BF16)

        return jnp.concatenate([ext[pl.ds(0, OWN), span], ext[pl.ds(2 * OWN, OWN), span]], axis=0)

    early = LENGTH - chunk
    sides = arrive(range(early // chunk))
    for number in range(LAGS // 2):
        partial[number] = products(sides, number, 0, early)
    sides = arrive([early // chunk])
    for number in range(LAGS // 2):
        total = partial[number] + products(sides, number, early, chunk)
        keep(0, number, total[:OWN])
        keep(2, number, total[OWN:])
    for pair in halos:
        for copy in pair:
            copy.wait_send()


def write_kernel(lagged, own_out, out_far, out, store_sem):
    def store(source, first, last):
        for group in range(TILE_ROWS):
            begin, end = max(0, first - group), min(TILES, last - group)
            if begin < end:
                place = (pl.ds(8 * group, 8), pl.ds(begin * OWN, (end - begin) * OWN))
                pltpu.make_async_copy(source.at[place], out_far.at[place], store_sem).start()

    store(own_out, TILE_ROWS, 2 * TILE_ROWS - 1)
    for first, last in ((0, TILE_ROWS), (2 * TILE_ROWS - 1, TILES + TILE_ROWS - 1)):
        finish(lagged, out, first, last)
        store(out, first, last)
    pltpu.make_async_copy(out, out_far, store_sem).wait()


def body(groups, inner, signal, fan_cut):
    operands = [signal, fan_cut.reshape(OWN, groups), *(jnp.asarray(table) for table in tables(groups))]
    operands = [pltpu.with_memory_space_constraint(array, pltpu.HBM) for array in operands]
    far = pl.BlockSpec(memory_space=pltpu.HBM)
    message = pltpu.VMEM((groups, 4, OWN), F32)
    lagged, own_out = pl.pallas_call(
        functools.partial(filter_kernel, groups, inner),
        out_shape=(pltpu.VMEM((3 * OWN * LAGS, OWN), F32), pltpu.VMEM((OWN, BAND * LAGS), F32)),
        in_specs=[far] * len(operands),
        out_specs=(pl.BlockSpec(memory_space=pltpu.VMEM),) * 2,
        scratch_shapes=[pltpu.VMEM(array.shape, array.dtype) for array in operands]
        + [pltpu.SemaphoreType.DMA((len(operands) + 1,))]
        + [message] * 4 + [pltpu.SemaphoreType.DMA] * 4 + [pltpu.SemaphoreType.DMA((2, 4))] * 2
        + [
            pltpu.VMEM((3 * OWN, LENGTH), BF16),
            pltpu.VMEM((LAGS * OWN, LENGTH), BF16),
            pltpu.VMEM((LAGS // 2, 2 * OWN, 2 * OWN), F32),
        ],
        compiler_params=pltpu.CompilerParams(
            collective_id=0, has_side_effects=True, vmem_limit_bytes=40 * 2**20
        ),
        name="fan_filter_products",
    )(*operands)
    lagged, own_out = (pltpu.with_memory_space_constraint(array, pltpu.VMEM) for array in (lagged, own_out))
    return pl.pallas_call(
        write_kernel,
        out_shape=jax.ShapeDtypeStruct((OWN, BAND * LAGS), F32),
        in_specs=[pl.BlockSpec(memory_space=pltpu.VMEM)] * 2,
        out_specs=far,
        scratch_shapes=[pltpu.VMEM((OWN, BAND * LAGS), F32), pltpu.SemaphoreType.DMA],
        compiler_params=pltpu.CompilerParams(vmem_limit_bytes=20 * 2**20),
        name="correlation_rows",
    )(lagged, own_out)


def solution(mesh):
    groups, inner = mesh.size, mesh.shape["cy"]
    return jax.shard_map(
        functools.partial(body, groups, inner),
        mesh=mesh,
        in_specs=(P(("cx", "cy"), None), P()),
        out_specs=P(("cx", "cy"), None),
        check_vma=False,
    )
```

```python
import functools
import math

import jax
import jax.numpy as jnp
import numpy as np
from jax import lax
from jax.experimental import pallas as pl
from jax.experimental.pallas import tpu as pltpu
from jax.sharding import PartitionSpec as P

BAND = 256
LAGS = 16
BINS = 256
OWN = 128
LENGTH = 1024
MESH = pl.DeviceIdType.MESH
F32 = jnp.float32
BF16 = jnp.bfloat16


def halves(table):
    high = table.astype(BF16)
    return high, (table - high.astype(np.float64)).astype(BF16)


def tables(groups):
    bin_index = np.arange(BINS, dtype=np.int64)
    angle = 2.0 * math.pi / LENGTH * (bin_index[:, None] * np.arange(LENGTH)[None, :] % LENGTH)
    pairs = np.stack([np.cos(angle), -np.sin(angle)], axis=1).reshape(groups, 2, 2, LENGTH)
    time = pairs.transpose(0, 2, 1, 3).reshape(2 * BINS, LENGTH)
    time[2] = np.cos(math.pi * np.arange(LENGTH))
    angle = 2.0 * math.pi / LENGTH * ((bin_index + BINS)[:, None] * np.arange(LENGTH)[None, :] % LENGTH)
    upper = np.concatenate([np.cos(angle), -np.sin(angle)])
    index = np.arange(groups)
    angle = 2.0 * math.pi / groups * (index[:, None] * index[None, :] % groups)
    re, im = np.cos(angle), -np.sin(angle)
    wide = np.block([[re, -im], [im, re]])
    angle = 2.0 * math.pi / (groups * OWN) * (index[:, None] * index[None, :])
    twist = np.stack([np.cos(angle), np.sin(angle)]).astype(np.float32)
    return np.stack(halves(time)), np.stack([*halves(wide), *halves(wide.T)]), twist, np.stack(halves(upper))


def dot(left, right, dims=((1,), (0,))):
    return lax.dot_general(left, right, (dims, ((), ())), preferred_element_type=F32)


def split(value):
    high = value.astype(BF16)
    return high, (value - high.astype(F32)).astype(BF16)


def dot_three(left, right):
    return dot(left[0], right[0]) + (dot(left[0], right[1]) + dot(left[1], right[0]))


def blocks(value):
    return value[:OWN, :OWN], value[:OWN, OWN:], value[OWN:, :OWN], value[OWN:, OWN:]


def join(a, b, c, d):
    return jnp.concatenate([jnp.concatenate([a, b], axis=1), jnp.concatenate([c, d], axis=1)], axis=0)


def least_cut(cut):
    row = lax.broadcasted_iota(jnp.int32, (OWN, OWN), 0)
    col = lax.broadcasted_iota(jnp.int32, (OWN, OWN), 1)
    mirror = (((row + col) % OWN) == 0).astype(F32).astype(BF16)
    reverse = ((row + col) == OWN - 1).astype(F32).astype(BF16)
    exact = cut.astype(F32).astype(BF16)
    across = dot(exact, mirror).astype(BF16)
    mirrored = jnp.where(col == 0, dot(mirror, across), dot(reverse, across))
    return jnp.maximum(cut.astype(F32), mirrored).T


TILES = BAND * LAGS // OWN
TILE_ROWS = OWN // 8


def finish(lagged, out, first, last):
    lane = lax.broadcasted_iota(jnp.int32, (8, OWN), 1)
    odd = [(lane // step) % 2 == 1 for step in (1, 2, 4)]
    for tile in range(first, last):
        rows = [lagged[pl.ds(tile * OWN + 8 * number, 8), :] for number in range(TILE_ROWS + 14)]
        for bit in range(3):
            gap = 2 << bit
            rows = [jnp.where(odd[bit], rows[spot + gap], rows[spot]) for spot in range(len(rows) - gap)]
        turned = jnp.concatenate(rows, axis=0).T
        for group in range(max(0, tile - TILES + 1), min(TILE_ROWS, tile + 1)):
            out[pl.ds(8 * group, 8), pl.ds((tile - group) * OWN, OWN)] = turned[8 * group:8 * group + 8]


def filter_kernel(
    groups, inner,
    signal_far, cut_far, time_far, wide_far, twist_far, upper_far,
    lagged, out,
    signal, cut, time, wide_all, twist, upper, load_sems,
    out_first, in_first, out_second, in_second,
    send_first, recv_first, send_second, recv_second, send_upper, recv_upper, send_lower, recv_lower,
    own_bins, upper_out, upper_in, upper_sides, lower_out, lower_in, ext, lags, sides,
):
    outer_at, inner_at = lax.axis_index("cx"), lax.axis_index("cy")
    me = outer_at * inner + inner_at

    def at(device):
        return (device // inner, device % inner)

    def peer(step):
        return lax.rem(me + step, groups)

    def visit_others(visit):
        high, mid, core = outer_at // 8, lax.rem(outer_at // 2, 4), lax.rem(outer_at, 2)
        top, low = inner_at // 4, lax.rem(inner_at, 4)
        highs, cores, tops = [8 * high, 8 - 8 * high], [core, 1 - core], [4 * top, 4 - 4 * top]

        def near(mid_step, low_step, combinations):
            mid_to, low_to = 2 * lax.rem(mid + mid_step, 4), lax.rem(low + low_step, 4)
            for flip_top, flip_high, flip_core in combinations:
                visit(highs[flip_high] + mid_to + cores[flip_core], tops[flip_top] + low_to)

        every = [(i, j, k) for i in (1, 0) for j in (1, 0) for k in (1, 0)]

        def far(number):
            return number + 2 - (number // 2) * (2 * number - 1)

        def block(index, carry):
            near(far(index // 4), far(lax.rem(index, 4)), every)
            return carry

        lax.fori_loop(0, 15, block, 0)
        near(0, 0, every[:-1])

    pairs = ((signal_far, signal), (time_far.at[0], time.at[0]), (time_far.at[1], time.at[1]),
             (cut_far, cut), (wide_far, wide_all), (twist_far, twist), (upper_far, upper))
    loads = [pltpu.make_async_copy(far, near, load_sems.at[number]) for number, (far, near) in enumerate(pairs)]
    for load in loads[:-1]:
        load.start()

    barrier = pltpu.get_barrier_semaphore()

    def greet(cx, cy):
        pl.semaphore_signal(barrier, inc=1, device_id=(cx, cy), device_id_type=MESH)

    visit_others(greet)
    loads[0].wait()
    time_high, time_low = time.at[0], time.at[1]
    own_high, own_low = split(signal[...])
    both = jnp.concatenate([own_high, own_low], axis=0)
    loads[1].wait()
    wide_sum = dot(time_high[...], both, ((1,), (1,)))
    loads[2].wait()
    spectrum = (wide_sum[:, :OWN] + wide_sum[:, OWN:]) + dot(time_low[...], own_high, ((1,), (1,)))
    out_first[...] = spectrum.reshape(groups, 4, OWN)

    loads[-1].start()
    pl.semaphore_wait(barrier, groups - 1)

    def exchange(outgoing, incoming, send_sem, recv_sem):
        def push(cx, cy):
            pltpu.make_async_remote_copy(
                src_ref=outgoing.at[cx * inner + cy],
                dst_ref=incoming.at[me],
                send_sem=send_sem,
                recv_sem=recv_sem,
                device_id=(cx, cy),
                device_id_type=MESH,
            ).start()

        visit_others(push)
        incoming[me] = outgoing[me]

    def settle(outgoing, incoming, send_sem, recv_sem):
        rest = pltpu.make_async_remote_copy(
            src_ref=outgoing.at[pl.ds(0, groups - 1)],
            dst_ref=incoming.at[pl.ds(0, groups - 1)],
            send_sem=send_sem,
            recv_sem=recv_sem,
            device_id=at(peer(1)),
            device_id_type=MESH,
        )
        rest.wait()

    exchange(out_first, in_first, send_first, recv_first)
    for load in loads[3:]:
        load.wait()
    lane = lax.broadcasted_iota(jnp.int32, (OWN, 2 * BINS), 1)
    own_bins[...] = spectrum.T * jnp.where((lane == 0) | (lane == 2), 1.0 / LENGTH, 2.0 / LENGTH)
    upper_sum = dot(both, upper[0], ((1,), (1,)))
    upper_sum = (upper_sum[:OWN] + upper_sum[OWN:]) + dot(own_high, upper[1], ((1,), (1,)))
    upper_out[...] = (upper_sum * (2.0 / LENGTH)).astype(BF16)

    def to_sides(outgoing, incoming, send_sems, recv_sems, rows):
        copies = [
            pltpu.make_async_remote_copy(
                src_ref=outgoing.at[rows], dst_ref=incoming.at[side, rows],
                send_sem=send_sems.at[side], recv_sem=recv_sems.at[side],
                device_id=at(peer(1 if side == 0 else groups - 1)), device_id_type=MESH,
            )
            for side in range(2)
        ]
        for copy in copies:
            copy.start()
        return copies

    early = to_sides(upper_out, upper_in, send_upper, recv_upper, pl.ds(0, OWN))
    cut_least = least_cut(cut[...])
    wide = (wide_all[0], wide_all[1])
    flip = (wide_all[2], wide_all[3])
    cosine, sine = twist[0], twist[1]
    settle(out_first, in_first, send_first, recv_first)

    rows = [in_first[:, part, :] for part in range(4)]
    rows[2] = rows[2] * jnp.where(me == 0, 0.0, 1.0)
    value = dot_three(wide, split(join(*rows)))
    re_a, re_b, im_a, im_b = blocks(value)
    value = join(
        re_a * cosine + im_a * sine, im_a * cosine - re_a * sine,
        re_b * cosine + im_b * sine, im_b * cosine - re_b * sine,
    )
    value = dot_three(split(value), flip)
    even = (2 * me).astype(F32)
    scale = -2.0 / (LENGTH * groups * OWN)
    keep_a = jnp.where(cut_least > even, jnp.where(me == 0, 0.5 * scale, scale), 0.0)
    keep_b = jnp.where(cut_least > even + 1.0, scale, 0.0)
    value = value * join(keep_a, keep_a, keep_b, keep_b)
    value = dot_three(split(value), wide)
    re_a, im_a, re_b, im_b = blocks(value)
    value = join(
        re_a * cosine - im_a * sine, re_b * cosine - im_b * sine,
        im_a * cosine + re_a * sine, im_b * cosine + re_b * sine,
    )
    value = dot_three(flip, split(value))
    for part, block in enumerate(blocks(value)):
        out_second[:, part, :] = block

    exchange(out_second, in_second, send_second, recv_second)
    for copy in early:
        copy.wait_recv()
    bins = upper_in[...].reshape(2 * OWN, 2 * BINS)
    upper_sides[...] = dot(bins, upper[0]) + dot(bins, upper[1])
    settle(out_second, in_second, send_second, recv_second)

    back = in_second[...].reshape(4 * groups, OWN).T
    lower_out[...] = (own_bins[...] + back).astype(BF16)
    half = OWN // 2
    late = [
        to_sides(lower_out, lower_in, send_lower.at[part], recv_lower.at[part], pl.ds(part * half, half))
        for part in range(2)
    ]
    back_high, back_low = split(back)
    both = jnp.concatenate([back_high, back_low], axis=0)
    chunk = 256
    for number in range(LENGTH // chunk):
        span = pl.ds(number * chunk, chunk)
        high, low = time_high[:, span], time_low[:, span]
        sums = dot(both, high)
        rejected = (sums[:OWN] + sums[OWN:]) + dot(back_high, low)
        ext[:, span] = (signal[:, span] + rejected).astype(BF16)
    own = ext[...] * jnp.asarray(1.0 / math.sqrt(LENGTH), BF16)
    for lag in range(LAGS):
        lags[pl.ds(lag * OWN, OWN), :] = own if lag == 0 else jnp.concatenate(
            [jnp.zeros((OWN, lag), BF16), own[:, :LENGTH - lag]], axis=1
        )

    def products(rows, number):
        return dot(rows, lags[pl.ds(number * 2 * OWN, 2 * OWN), :], ((1,), (1,)))

    def keep(first_row, number, values):
        for side in range(2):
            begin = first_row * LAGS + 2 * number + side
            lagged[pl.ds(begin, values.shape[0], stride=LAGS), :] = values[:, side * OWN:(side + 1) * OWN]

    middle = ext[...]
    for number in range(LAGS // 2):
        keep(OWN, number, products(middle, number))
    finish(lagged, out, TILE_ROWS, 2 * TILE_ROWS - 1)

    row = lax.broadcasted_iota(jnp.int32, (OWN, chunk), 0)
    inside = jnp.where(row < half, (me > 0).astype(F32), (me < groups - 1).astype(F32))
    for part in range(2):
        for copy in late[part]:
            copy.wait_recv()
        rows = pl.ds(part * half, half)
        bins = jnp.concatenate([lower_in[0, rows, :], lower_in[1, rows, :]], axis=0)
        for number in range(LENGTH // chunk):
            span = pl.ds(number * chunk, chunk)
            upper_part = jnp.concatenate(
                [upper_sides[rows, span], upper_sides[pl.ds(OWN + part * half, half), span]], axis=0
            )
            value = dot(bins, time_high[:, span]) + dot(bins, time_low[:, span]) + upper_part
            sides[:, span] = (value * inside).astype(BF16)
        middle = sides[...]
        for number in range(LAGS // 2):
            values = products(middle, number)
            keep(part * half, number, values[:half])
            keep(2 * OWN + part * half, number, values[half:])
    for copy in early + late[0] + late[1]:
        copy.wait_send()


def write_kernel(lagged, own_out, out_far, out, store_sem):
    def store(source, first, last):
        for group in range(TILE_ROWS):
            begin, end = max(0, first - group), min(TILES, last - group)
            if begin < end:
                place = (pl.ds(8 * group, 8), pl.ds(begin * OWN, (end - begin) * OWN))
                pltpu.make_async_copy(source.at[place], out_far.at[place], store_sem).start()

    store(own_out, TILE_ROWS, 2 * TILE_ROWS - 1)
    for first, last in ((0, TILE_ROWS), (2 * TILE_ROWS - 1, TILES + TILE_ROWS - 1)):
        finish(lagged, out, first, last)
        store(out, first, last)
    pltpu.make_async_copy(out, out_far, store_sem).wait()


def body(groups, inner, signal, fan_cut):
    operands = [signal, fan_cut.reshape(OWN, groups), *(jnp.asarray(table) for table in tables(groups))]
    operands = [pltpu.with_memory_space_constraint(array, pltpu.HBM) for array in operands]
    far = pl.BlockSpec(memory_space=pltpu.HBM)
    message = pltpu.VMEM((groups, 4, OWN), F32)
    lagged, own_out = pl.pallas_call(
        functools.partial(filter_kernel, groups, inner),
        out_shape=(pltpu.VMEM((3 * OWN * LAGS, OWN), F32), pltpu.VMEM((OWN, BAND * LAGS), F32)),
        in_specs=[far] * len(operands),
        out_specs=(pl.BlockSpec(memory_space=pltpu.VMEM),) * 2,
        scratch_shapes=[pltpu.VMEM(array.shape, array.dtype) for array in operands]
        + [pltpu.SemaphoreType.DMA((len(operands) + 1,))]
        + [message] * 4 + [pltpu.SemaphoreType.DMA] * 4 + [pltpu.SemaphoreType.DMA((2,))] * 2 + [pltpu.SemaphoreType.DMA((2, 2))] * 2
        + [
            pltpu.VMEM((OWN, 2 * BINS), F32),
            pltpu.VMEM((OWN, 2 * BINS), BF16),
            pltpu.VMEM((2, OWN, 2 * BINS), BF16),
            pltpu.VMEM((2 * OWN, LENGTH), F32),
            pltpu.VMEM((OWN, 2 * BINS), BF16),
            pltpu.VMEM((2, OWN, 2 * BINS), BF16),
            pltpu.VMEM((OWN, LENGTH), BF16),
            pltpu.VMEM((LAGS * OWN, LENGTH), BF16),
            pltpu.VMEM((OWN, LENGTH), BF16),
        ],
        compiler_params=pltpu.CompilerParams(
            collective_id=0, has_side_effects=True, vmem_limit_bytes=40 * 2**20
        ),
        name="fan_filter_products",
    )(*operands)
    lagged, own_out = (pltpu.with_memory_space_constraint(array, pltpu.VMEM) for array in (lagged, own_out))
    return pl.pallas_call(
        write_kernel,
        out_shape=jax.ShapeDtypeStruct((OWN, BAND * LAGS), F32),
        in_specs=[pl.BlockSpec(memory_space=pltpu.VMEM)] * 2,
        out_specs=far,
        scratch_shapes=[pltpu.VMEM((OWN, BAND * LAGS), F32), pltpu.SemaphoreType.DMA],
        compiler_params=pltpu.CompilerParams(vmem_limit_bytes=20 * 2**20),
        name="correlation_rows",
    )(lagged, own_out)


def solution(mesh):
    groups, inner = mesh.size, mesh.shape["cy"]
    return jax.shard_map(
        functools.partial(body, groups, inner),
        mesh=mesh,
        in_specs=(P(("cx", "cy"), None), P()),
        out_specs=P(("cx", "cy"), None),
        check_vma=False,
    )
```

```python
import functools
import math

import jax
import jax.numpy as jnp
import numpy as np
from jax import lax
from jax.experimental import pallas as pl
from jax.experimental.pallas import tpu as pltpu
from jax.sharding import PartitionSpec as P

BAND = 256
LAGS = 16
BINS = 256
OWN = 128
LENGTH = 1024
MESH = pl.DeviceIdType.MESH
F32 = jnp.float32
BF16 = jnp.bfloat16


def halves(table):
    high = table.astype(BF16)
    return high, (table - high.astype(np.float64)).astype(BF16)


def tables(groups):
    bin_index = np.arange(BINS, dtype=np.int64)
    angle = 2.0 * math.pi / LENGTH * (bin_index[:, None] * np.arange(LENGTH)[None, :] % LENGTH)
    pairs = np.stack([np.cos(angle), -np.sin(angle)], axis=1).reshape(groups, 2, 2, LENGTH)
    time = pairs.transpose(2, 1, 0, 3).reshape(2 * BINS, LENGTH)
    time[2 * groups] = np.cos(math.pi * np.arange(LENGTH))
    angle = 2.0 * math.pi / LENGTH * ((bin_index + BINS)[:, None] * np.arange(LENGTH)[None, :] % LENGTH)
    upper = np.concatenate([np.cos(angle), -np.sin(angle)])
    index = np.arange(groups)
    angle = 2.0 * math.pi / groups * (index[:, None] * index[None, :] % groups)
    re, im = np.cos(angle), -np.sin(angle)
    wide = np.block([[re, -im], [im, re]])
    angle = 2.0 * math.pi / (groups * OWN) * (index[:, None] * index[None, :])
    twist = np.stack([np.cos(angle), np.sin(angle)]).astype(np.float32)
    return np.stack(halves(time)), np.stack([*halves(wide), *halves(wide.T)]), twist, np.stack(halves(upper))


def dot(left, right, dims=((1,), (0,))):
    return lax.dot_general(left, right, (dims, ((), ())), preferred_element_type=F32)


def split(value):
    high = value.astype(BF16)
    return high, (value - high.astype(F32)).astype(BF16)


def dot_three(left, right):
    return dot(left[0], right[0]) + (dot(left[0], right[1]) + dot(left[1], right[0]))


def blocks(value):
    return value[:OWN, :OWN], value[:OWN, OWN:], value[OWN:, :OWN], value[OWN:, OWN:]


def join(a, b, c, d):
    return jnp.concatenate([jnp.concatenate([a, b], axis=1), jnp.concatenate([c, d], axis=1)], axis=0)


def least_cut(cut):
    row = lax.broadcasted_iota(jnp.int32, (OWN, OWN), 0)
    col = lax.broadcasted_iota(jnp.int32, (OWN, OWN), 1)
    mirror = (((row + col) % OWN) == 0).astype(F32).astype(BF16)
    reverse = ((row + col) == OWN - 1).astype(F32).astype(BF16)
    exact = cut.astype(F32).astype(BF16)
    across = dot(exact, mirror).astype(BF16)
    mirrored = jnp.where(col == 0, dot(mirror, across), dot(reverse, across))
    return jnp.maximum(cut.astype(F32), mirrored).T


TILES = BAND * LAGS // OWN
TILE_ROWS = OWN // 8
PACK = 16


def finish(lagged, out, first, last):
    lane = lax.broadcasted_iota(jnp.int32, (8, OWN), 1)
    odd = [(lane // step) % 2 == 1 for step in (1, 2, 4)]
    for tile in range(first, last):
        rows = [lagged[pl.ds(tile * OWN + 8 * number, 8), :] for number in range(TILE_ROWS + 14)]
        for bit in range(3):
            gap = 2 << bit
            rows = [jnp.where(odd[bit], rows[spot + gap], rows[spot]) for spot in range(len(rows) - gap)]
        turned = jnp.concatenate(rows, axis=0).T
        for group in range(max(0, tile - TILES + 1), min(TILE_ROWS, tile + 1)):
            out[pl.ds(8 * group, 8), pl.ds((tile - group) * OWN, OWN)] = turned[8 * group:8 * group + 8]


def filter_kernel(
    groups, inner,
    signal_far, cut_far, time_far, wide_far, twist_far, upper_far,
    lagged,
    signal, cut, time, wide_all, twist, upper, load_sems,
    out_first, in_first, out_second, in_second,
    send_first, recv_first, send_second, recv_second, send_upper, recv_upper,
    upper_out, upper_in, upper_sides, packed, ext, lags,
):
    outer_at, inner_at = lax.axis_index("cx"), lax.axis_index("cy")
    me = outer_at * inner + inner_at

    def at(device):
        return (device // inner, device % inner)

    def peer(step):
        return lax.rem(me + step, groups)

    def visit_others(visit):
        high, mid, core = outer_at // 8, lax.rem(outer_at // 2, 4), lax.rem(outer_at, 2)
        top, low = inner_at // 4, lax.rem(inner_at, 4)
        highs, cores, tops = [8 * high, 8 - 8 * high], [core, 1 - core], [4 * top, 4 - 4 * top]

        def near(mid_step, low_step, combinations):
            mid_to, low_to = 2 * lax.rem(mid + mid_step, 4), lax.rem(low + low_step, 4)
            for flip_top, flip_high, flip_core in combinations:
                visit(highs[flip_high] + mid_to + cores[flip_core], tops[flip_top] + low_to)

        every = [(i, j, k) for i in (1, 0) for j in (1, 0) for k in (1, 0)]

        def far(number):
            return number + 2 - (number // 2) * (2 * number - 1)

        def block(index, carry):
            near(far(index // 4), far(lax.rem(index, 4)), every)
            return carry

        lax.fori_loop(0, 15, block, 0)
        near(0, 0, every[:-1])

    pairs = ((signal_far, signal), (time_far.at[0], time.at[0]), (time_far.at[1], time.at[1]),
             (cut_far, cut), (wide_far, wide_all), (twist_far, twist), (upper_far, upper))
    loads = [pltpu.make_async_copy(far, near, load_sems.at[number]) for number, (far, near) in enumerate(pairs)]
    for load in loads[:-1]:
        load.start()

    barrier = pltpu.get_barrier_semaphore()

    def greet(cx, cy):
        pl.semaphore_signal(barrier, inc=1, device_id=(cx, cy), device_id_type=MESH)

    visit_others(greet)
    loads[0].wait()
    time_high, time_low = time.at[0], time.at[1]
    own_high, own_low = split(signal[...])
    both = jnp.concatenate([own_high, own_low], axis=0)
    loads[1].wait()
    wide_sum = dot(time_high[...], both, ((1,), (1,)))
    loads[2].wait()
    spectrum = (wide_sum[:, :OWN] + wide_sum[:, OWN:]) + dot(time_low[...], own_high, ((1,), (1,)))
    for part in range(4):
        out_first[:, part, :] = spectrum[part * OWN:(part + 1) * OWN]

    loads[-1].start()
    pl.semaphore_wait(barrier, groups - 1)

    def exchange(outgoing, incoming, send_sem, recv_sem):
        def push(cx, cy):
            pltpu.make_async_remote_copy(
                src_ref=outgoing.at[cx * inner + cy],
                dst_ref=incoming.at[me],
                send_sem=send_sem,
                recv_sem=recv_sem,
                device_id=(cx, cy),
                device_id_type=MESH,
            ).start()

        visit_others(push)
        incoming[me] = outgoing[me]

    def settle(outgoing, incoming, send_sem, recv_sem):
        rest = pltpu.make_async_remote_copy(
            src_ref=outgoing.at[pl.ds(0, groups - 1)],
            dst_ref=incoming.at[pl.ds(0, groups - 1)],
            send_sem=send_sem,
            recv_sem=recv_sem,
            device_id=at(peer(1)),
            device_id_type=MESH,
        )
        rest.wait()

    exchange(out_first, in_first, send_first, recv_first)
    for load in loads[3:]:
        load.wait()
    upper_sum = dot(both, upper[0], ((1,), (1,)))
    upper_sum = (upper_sum[:OWN] + upper_sum[OWN:]) + dot(own_high, upper[1], ((1,), (1,)))
    upper_out[...] = (upper_sum * (2.0 / LENGTH)).astype(BF16)

    early = [
        pltpu.make_async_remote_copy(
            src_ref=upper_out, dst_ref=upper_in.at[side],
            send_sem=send_upper.at[side], recv_sem=recv_upper.at[side],
            device_id=at(peer(1 if side == 0 else groups - 1)), device_id_type=MESH,
        )
        for side in range(2)
    ]
    for copy in early:
        copy.start()
    cut_least = least_cut(cut[...])
    wide = (wide_all[0], wide_all[1])
    flip = (wide_all[2], wide_all[3])
    cosine, sine = twist[0], twist[1]
    settle(out_first, in_first, send_first, recv_first)

    rows = [in_first[:, part, :] for part in range(4)]
    value = dot_three(wide, split(join(rows[0], rows[1], rows[2] * jnp.where(me == 0, 0.0, 1.0), rows[3])))
    re_a, re_b, im_a, im_b = blocks(value)
    value = join(
        re_a * cosine + im_a * sine, im_a * cosine - re_a * sine,
        re_b * cosine + im_b * sine, im_b * cosine - re_b * sine,
    )
    value = dot_three(split(value), flip)
    even = (2 * me).astype(F32)
    scale = -2.0 / (LENGTH * groups * OWN)
    keep_a = jnp.where(cut_least > even, jnp.where(me == 0, 0.5 * scale, scale), 0.0)
    keep_b = jnp.where(cut_least > even + 1.0, scale, 0.0)
    value = value * join(keep_a, keep_a, keep_b, keep_b)
    value = dot_three(split(value), wide)
    re_a, im_a, re_b, im_b = blocks(value)
    value = join(
        re_a * cosine - im_a * sine, re_b * cosine - im_b * sine,
        im_a * cosine + re_a * sine, im_b * cosine + re_b * sine,
    )
    value = dot_three(flip, split(value))
    for part, block in enumerate(blocks(value)):
        weight = 2.0 / LENGTH if part % 2 else jnp.where(me == 0, 1.0 / LENGTH, 2.0 / LENGTH)
        kept = rows[part] * weight + block
        for first, array in (
            (PACK, block), (PACK + 4, block - block.astype(BF16).astype(F32)), (2 * PACK + 8, kept), (12, kept),
        ):
            packed[pl.ds(first + part, groups, stride=PACK), :] = array
    for first in (PACK + 8, PACK * groups + 12):
        packed[pl.ds(first, 4), :] = jnp.zeros((4, OWN), F32)
    out_second[...] = packed[pl.ds(PACK, PACK * groups), :].astype(BF16).reshape(groups, PACK, OWN)

    exchange(out_second, in_second, send_second, recv_second)
    for copy in early:
        copy.wait_recv()
    bins = upper_in[...].reshape(2 * OWN, 2 * BINS)
    row = lax.broadcasted_iota(jnp.int32, (2 * OWN, LENGTH), 0)
    inside = jnp.where(row < OWN, (me > 0).astype(F32), (me < groups - 1).astype(F32))
    upper_sides[...] = (dot(bins, upper[0]) + dot(bins, upper[1])) * inside
    settle(out_second, in_second, send_second, recv_second)

    packed[pl.ds(0, PACK * groups), :] = in_second[...].astype(F32).reshape(PACK * groups, OWN)

    def turn(*firsts):
        parts = [[packed[pl.ds(first + part, groups, stride=PACK), :] for first in firsts] for part in range(4)]
        return jnp.concatenate([sum(part[1:], part[0]).T for part in parts], axis=1)

    back_high, back_low = split(turn(0, 4))
    all_bins = jnp.concatenate([back_high, back_low, turn(8).astype(BF16), turn(12).astype(BF16)], axis=0)
    chunk = 256
    for number in range(LENGTH // chunk):
        span = pl.ds(number * chunk, chunk)
        sums = dot(all_bins, time_high[:, span])
        rejected = (sums[:OWN] + sums[OWN:2 * OWN]) + dot(back_high, time_low[:, span])
        ext[pl.ds(OWN, OWN), span] = (signal[:, span] + rejected).astype(BF16)
        ext[pl.ds(0, OWN), span] = (upper_sides[pl.ds(0, OWN), span] + sums[2 * OWN:3 * OWN]).astype(BF16)
        ext[pl.ds(2 * OWN, OWN), span] = (upper_sides[pl.ds(OWN, OWN), span] + sums[3 * OWN:]).astype(BF16)
    own = ext[pl.ds(OWN, OWN), :] * jnp.asarray(1.0 / math.sqrt(LENGTH), BF16)
    for lag in range(LAGS):
        lags[pl.ds(lag * OWN, OWN), :] = own if lag == 0 else jnp.concatenate(
            [jnp.zeros((OWN, lag), BF16), own[:, :LENGTH - lag]], axis=1
        )

    everything = ext[...]
    for number in range(LAGS // 2):
        values = dot(everything, lags[pl.ds(number * 2 * OWN, 2 * OWN), :], ((1,), (1,)))
        for side in range(2):
            lagged[pl.ds(2 * number + side, 3 * OWN, stride=LAGS), :] = values[:, side * OWN:(side + 1) * OWN]
    for copy in early:
        copy.wait_send()


def write_kernel(lagged, out_far, out, store_sem):
    done = 0
    for last in range(TILE_ROWS + TILES // 4 - 1, TILE_ROWS + TILES, TILES // 4):
        finish(lagged, out, done, last)
        done = last
        columns = pl.ds((last - TILE_ROWS + 1 - TILES // 4) * OWN, TILES // 4 * OWN)
        pltpu.make_async_copy(out.at[:, columns], out_far.at[:, columns], store_sem).start()
    pltpu.make_async_copy(out, out_far, store_sem).wait()


def body(groups, inner, signal, fan_cut):
    operands = [signal, fan_cut.reshape(OWN, groups), *(jnp.asarray(table) for table in tables(groups))]
    operands = [pltpu.with_memory_space_constraint(array, pltpu.HBM) for array in operands]
    far = pl.BlockSpec(memory_space=pltpu.HBM)
    messages = [pltpu.VMEM((groups, 4, OWN), F32)] * 2 + [pltpu.VMEM((groups, PACK, OWN), BF16)] * 2
    lagged = pl.pallas_call(
        functools.partial(filter_kernel, groups, inner),
        out_shape=pltpu.VMEM((3 * OWN * LAGS, OWN), F32),
        in_specs=[far] * len(operands),
        out_specs=pl.BlockSpec(memory_space=pltpu.VMEM),
        scratch_shapes=[pltpu.VMEM(array.shape, array.dtype) for array in operands]
        + [pltpu.SemaphoreType.DMA((len(operands) + 1,))]
        + messages + [pltpu.SemaphoreType.DMA] * 4 + [pltpu.SemaphoreType.DMA((2,))] * 2
        + [
            pltpu.VMEM((OWN, 2 * BINS), BF16),
            pltpu.VMEM((2, OWN, 2 * BINS), BF16),
            pltpu.VMEM((2 * OWN, LENGTH), F32),
            pltpu.VMEM((PACK * (groups + 2), OWN), F32),
            pltpu.VMEM((3 * OWN, LENGTH), BF16),
            pltpu.VMEM((LAGS * OWN, LENGTH), BF16),
        ],
        compiler_params=pltpu.CompilerParams(
            collective_id=0, has_side_effects=True, vmem_limit_bytes=40 * 2**20
        ),
        name="fan_filter_products",
    )(*operands)
    lagged = pltpu.with_memory_space_constraint(lagged, pltpu.VMEM)
    return pl.pallas_call(
        write_kernel,
        out_shape=jax.ShapeDtypeStruct((OWN, BAND * LAGS), F32),
        in_specs=[pl.BlockSpec(memory_space=pltpu.VMEM)],
        out_specs=far,
        scratch_shapes=[pltpu.VMEM((OWN, BAND * LAGS), F32), pltpu.SemaphoreType.DMA],
        compiler_params=pltpu.CompilerParams(vmem_limit_bytes=20 * 2**20),
        name="correlation_rows",
    )(lagged)


def solution(mesh):
    groups, inner = mesh.size, mesh.shape["cy"]
    return jax.shard_map(
        functools.partial(body, groups, inner),
        mesh=mesh,
        in_specs=(P(("cx", "cy"), None), P()),
        out_specs=P(("cx", "cy"), None),
        check_vma=False,
    )
```

```python
import functools
import math

import jax
import jax.numpy as jnp
import numpy as np
from jax import lax
from jax.experimental import pallas as pl
from jax.experimental.pallas import tpu as pltpu
from jax.sharding import PartitionSpec as P

BAND = 256
LAGS = 16
BINS = 256
OWN = 128
LENGTH = 1024
MESH = pl.DeviceIdType.MESH
F32 = jnp.float32
BF16 = jnp.bfloat16


def halves(table):
    high = table.astype(BF16)
    return high, (table - high.astype(np.float64)).astype(BF16)


def tables(groups):
    bin_index = np.arange(BINS, dtype=np.int64)
    angle = 2.0 * math.pi / LENGTH * (bin_index[:, None] * np.arange(LENGTH)[None, :] % LENGTH)
    pairs = np.stack([np.cos(angle), -np.sin(angle)], axis=1).reshape(groups, 2, 2, LENGTH)
    time = pairs.transpose(2, 1, 0, 3).reshape(2 * BINS, LENGTH)
    time[2 * groups] = np.cos(math.pi * np.arange(LENGTH))
    angle = 2.0 * math.pi / LENGTH * ((bin_index + BINS)[:, None] * np.arange(LENGTH)[None, :] % LENGTH)
    upper = np.concatenate([np.cos(angle), -np.sin(angle)])
    index = np.arange(groups)
    angle = 2.0 * math.pi / groups * (index[:, None] * index[None, :] % groups)
    re, im = np.cos(angle), -np.sin(angle)
    wide = np.block([[re, -im], [im, re]])
    angle = 2.0 * math.pi / (groups * OWN) * (index[:, None] * index[None, :])
    twist = np.stack([np.cos(angle), np.sin(angle)]).astype(np.float32)
    return np.stack(halves(time)), np.stack([*halves(wide), *halves(wide.T)]), twist, np.stack(halves(upper))


def dot(left, right, dims=((1,), (0,))):
    return lax.dot_general(left, right, (dims, ((), ())), preferred_element_type=F32)


def split(value):
    high = value.astype(BF16)
    return high, (value - high.astype(F32)).astype(BF16)


def dot_three(left, right):
    return dot(left[0], right[0]) + (dot(left[0], right[1]) + dot(left[1], right[0]))


def blocks(value):
    return value[:OWN, :OWN], value[:OWN, OWN:], value[OWN:, :OWN], value[OWN:, OWN:]


def join(a, b, c, d):
    return jnp.concatenate([jnp.concatenate([a, b], axis=1), jnp.concatenate([c, d], axis=1)], axis=0)


def least_cut(cut):
    row = lax.broadcasted_iota(jnp.int32, (OWN, OWN), 0)
    col = lax.broadcasted_iota(jnp.int32, (OWN, OWN), 1)
    mirror = (((row + col) % OWN) == 0).astype(F32).astype(BF16)
    reverse = ((row + col) == OWN - 1).astype(F32).astype(BF16)
    exact = cut.astype(F32).astype(BF16)
    across = dot(exact, mirror).astype(BF16)
    mirrored = jnp.where(col == 0, dot(mirror, across), dot(reverse, across))
    return jnp.maximum(cut.astype(F32), mirrored).T


TILES = BAND * LAGS // OWN
TILE_ROWS = OWN // 8
PACK = 16


def finish(lagged, out, first, last):
    lane = lax.broadcasted_iota(jnp.int32, (8, OWN), 1)
    odd = [(lane // step) % 2 == 1 for step in (1, 2, 4)]
    for tile in range(first, last):
        rows = [lagged[pl.ds(tile * OWN + 8 * number, 8), :] for number in range(TILE_ROWS + 14)]
        for bit in range(3):
            gap = 2 << bit
            rows = [jnp.where(odd[bit], rows[spot + gap], rows[spot]) for spot in range(len(rows) - gap)]
        turned = jnp.concatenate(rows, axis=0).T
        for group in range(max(0, tile - TILES + 1), min(TILE_ROWS, tile + 1)):
            out[pl.ds(8 * group, 8), pl.ds((tile - group) * OWN, OWN)] = turned[8 * group:8 * group + 8]


def filter_kernel(
    groups, inner,
    signal_far, cut_far, time_far, wide_far, twist_far, upper_far,
    lagged,
    signal, cut, time, wide_all, twist, upper, load_sems,
    out_first, in_first, out_second, in_second,
    send_first, recv_first, send_second, recv_second, send_upper, recv_upper,
    upper_out, upper_in, upper_sides, packed, ext, lags,
):
    outer_at, inner_at = lax.axis_index("cx"), lax.axis_index("cy")
    me = outer_at * inner + inner_at

    def at(device):
        return (device // inner, device % inner)

    def peer(step):
        return lax.rem(me + step, groups)

    def visit_others(visit):
        high, mid, core = outer_at // 8, lax.rem(outer_at // 2, 4), lax.rem(outer_at, 2)
        top, low = inner_at // 4, lax.rem(inner_at, 4)
        highs, cores, tops = (8 * high, 8 - 8 * high), (core, 1 - core), (4 * top, 4 - 4 * top)
        mids = [2 * lax.rem(mid + step, 4) for step in range(4)]
        lows = [lax.rem(low + step, 4) for step in range(4)]
        far = ((2, 2), (1, 3), (3, 1), (1, 1), (3, 3), (2, 1), (1, 2), (2, 3), (3, 2))
        near = ((2, 0), (0, 2), (1, 0), (0, 3), (3, 0), (0, 1), (0, 0))

        def block(index, carry, steps):
            cx = jnp.where(lax.rem(index // 2, 2) == 0, highs[1], highs[0])
            cx = cx + jnp.where(lax.rem(index, 2) == 0, cores[1], cores[0])
            cy = jnp.where(index // 4 == 0, tops[1], tops[0])
            for mid_step, low_step in steps:
                visit(cx + mids[mid_step], cy + lows[low_step])
            return carry

        lax.fori_loop(0, 8, functools.partial(block, steps=far), 0)
        lax.fori_loop(0, 7, functools.partial(block, steps=near), 0)
        block(7, 0, near[:-1])

    pairs = ((signal_far, signal), (time_far.at[0], time.at[0]), (time_far.at[1], time.at[1]),
             (cut_far, cut), (wide_far, wide_all), (twist_far, twist), (upper_far, upper))
    loads = [pltpu.make_async_copy(far, near, load_sems.at[number]) for number, (far, near) in enumerate(pairs)]
    for load in loads[:-1]:
        load.start()

    barrier = pltpu.get_barrier_semaphore()

    def greet(cx, cy):
        pl.semaphore_signal(barrier, inc=1, device_id=(cx, cy), device_id_type=MESH)

    visit_others(greet)
    loads[0].wait()
    time_high, time_low = time.at[0], time.at[1]
    own_high, own_low = split(signal[...])
    both = jnp.concatenate([own_high, own_low], axis=0)
    loads[1].wait()
    wide_sum = dot(time_high[...], both, ((1,), (1,)))
    loads[2].wait()
    spectrum = (wide_sum[:, :OWN] + wide_sum[:, OWN:]) + dot(time_low[...], own_high, ((1,), (1,)))
    for part in range(4):
        out_first[:, part, :] = spectrum[part * OWN:(part + 1) * OWN]

    loads[-1].start()
    pl.semaphore_wait(barrier, groups - 1)

    def exchange(outgoing, incoming, send_sem, recv_sem):
        def push(cx, cy):
            pltpu.make_async_remote_copy(
                src_ref=outgoing.at[cx * inner + cy],
                dst_ref=incoming.at[me],
                send_sem=send_sem,
                recv_sem=recv_sem,
                device_id=(cx, cy),
                device_id_type=MESH,
            ).start()

        visit_others(push)
        incoming[me] = outgoing[me]

    def settle(outgoing, incoming, send_sem, recv_sem):
        rest = pltpu.make_async_remote_copy(
            src_ref=outgoing.at[pl.ds(0, groups - 1)],
            dst_ref=incoming.at[pl.ds(0, groups - 1)],
            send_sem=send_sem,
            recv_sem=recv_sem,
            device_id=at(peer(1)),
            device_id_type=MESH,
        )
        rest.wait()

    exchange(out_first, in_first, send_first, recv_first)
    for load in loads[3:]:
        load.wait()
    upper_sum = dot(both, upper[0], ((1,), (1,)))
    upper_sum = (upper_sum[:OWN] + upper_sum[OWN:]) + dot(own_high, upper[1], ((1,), (1,)))
    upper_out[...] = (upper_sum * (2.0 / LENGTH)).astype(BF16)

    early = [
        pltpu.make_async_remote_copy(
            src_ref=upper_out, dst_ref=upper_in.at[side],
            send_sem=send_upper.at[side], recv_sem=recv_upper.at[side],
            device_id=at(peer(1 if side == 0 else groups - 1)), device_id_type=MESH,
        )
        for side in range(2)
    ]
    for copy in early:
        copy.start()
    cut_least = least_cut(cut[...])
    wide = (wide_all[0], wide_all[1])
    flip = (wide_all[2], wide_all[3])
    cosine, sine = twist[0], twist[1]
    settle(out_first, in_first, send_first, recv_first)

    rows = [in_first[:, part, :] for part in range(4)]
    value = dot_three(wide, split(join(rows[0], rows[1], rows[2] * jnp.where(me == 0, 0.0, 1.0), rows[3])))
    re_a, re_b, im_a, im_b = blocks(value)
    value = join(
        re_a * cosine + im_a * sine, im_a * cosine - re_a * sine,
        re_b * cosine + im_b * sine, im_b * cosine - re_b * sine,
    )
    value = dot_three(split(value), flip)
    even = (2 * me).astype(F32)
    scale = -2.0 / (LENGTH * groups * OWN)
    keep_a = jnp.where(cut_least > even, jnp.where(me == 0, 0.5 * scale, scale), 0.0)
    keep_b = jnp.where(cut_least > even + 1.0, scale, 0.0)
    value = value * join(keep_a, keep_a, keep_b, keep_b)
    value = dot_three(split(value), wide)
    re_a, im_a, re_b, im_b = blocks(value)
    value = join(
        re_a * cosine - im_a * sine, re_b * cosine - im_b * sine,
        im_a * cosine + re_a * sine, im_b * cosine + re_b * sine,
    )
    value = dot_three(flip, split(value))
    for part, block in enumerate(blocks(value)):
        weight = 2.0 / LENGTH if part % 2 else jnp.where(me == 0, 1.0 / LENGTH, 2.0 / LENGTH)
        kept = rows[part] * weight + block
        for first, array in (
            (PACK, block), (PACK + 4, block - block.astype(BF16).astype(F32)), (2 * PACK + 8, kept), (12, kept),
        ):
            packed[pl.ds(first + part, groups, stride=PACK), :] = array
    for first in (PACK + 8, PACK * groups + 12):
        packed[pl.ds(first, 4), :] = jnp.zeros((4, OWN), F32)
    out_second[...] = packed[pl.ds(PACK, PACK * groups), :].astype(BF16).reshape(groups, PACK, OWN)

    exchange(out_second, in_second, send_second, recv_second)
    for copy in early:
        copy.wait_recv()
    bins = upper_in[...].reshape(2 * OWN, 2 * BINS)
    row = lax.broadcasted_iota(jnp.int32, (2 * OWN, LENGTH), 0)
    inside = jnp.where(row < OWN, (me > 0).astype(F32), (me < groups - 1).astype(F32))
    upper_sides[...] = (dot(bins, upper[0]) + dot(bins, upper[1])) * inside
    settle(out_second, in_second, send_second, recv_second)

    packed[pl.ds(0, PACK * groups), :] = in_second[...].astype(F32).reshape(PACK * groups, OWN)

    def turn(*firsts):
        parts = [[packed[pl.ds(first + part, groups, stride=PACK), :] for first in firsts] for part in range(4)]
        return jnp.concatenate([sum(part[1:], part[0]).T for part in parts], axis=1)

    back_high, back_low = split(turn(0, 4))
    all_bins = jnp.concatenate([back_high, back_low, turn(8).astype(BF16), turn(12).astype(BF16)], axis=0)
    chunk = 256
    for number in range(LENGTH // chunk):
        span = pl.ds(number * chunk, chunk)
        sums = dot(all_bins, time_high[:, span])
        rejected = (sums[:OWN] + sums[OWN:2 * OWN]) + dot(back_high, time_low[:, span])
        ext[pl.ds(OWN, OWN), span] = (signal[:, span] + rejected).astype(BF16)
        ext[pl.ds(0, OWN), span] = (upper_sides[pl.ds(0, OWN), span] + sums[2 * OWN:3 * OWN]).astype(BF16)
        ext[pl.ds(2 * OWN, OWN), span] = (upper_sides[pl.ds(OWN, OWN), span] + sums[3 * OWN:]).astype(BF16)
    own = ext[pl.ds(OWN, OWN), :] * jnp.asarray(1.0 / math.sqrt(LENGTH), BF16)
    for lag in range(LAGS):
        lags[pl.ds(lag * OWN, OWN), :] = own if lag == 0 else jnp.concatenate(
            [jnp.zeros((OWN, lag), BF16), own[:, :LENGTH - lag]], axis=1
        )

    everything = ext[...]
    for number in range(LAGS // 2):
        values = dot(everything, lags[pl.ds(number * 2 * OWN, 2 * OWN), :], ((1,), (1,)))
        for side in range(2):
            lagged[pl.ds(2 * number + side, 3 * OWN, stride=LAGS), :] = values[:, side * OWN:(side + 1) * OWN]
    for copy in early:
        copy.wait_send()


def write_kernel(lagged, out_far, out, store_sem):
    done = 0
    for last in range(TILE_ROWS + TILES // 4 - 1, TILE_ROWS + TILES, TILES // 4):
        finish(lagged, out, done, last)
        done = last
        columns = pl.ds((last - TILE_ROWS + 1 - TILES // 4) * OWN, TILES // 4 * OWN)
        pltpu.make_async_copy(out.at[:, columns], out_far.at[:, columns], store_sem).start()
    pltpu.make_async_copy(out, out_far, store_sem).wait()


def body(groups, inner, signal, fan_cut):
    operands = [signal, fan_cut.reshape(OWN, groups), *(jnp.asarray(table) for table in tables(groups))]
    operands = [pltpu.with_memory_space_constraint(array, pltpu.HBM) for array in operands]
    far = pl.BlockSpec(memory_space=pltpu.HBM)
    messages = [pltpu.VMEM((groups, 4, OWN), F32)] * 2 + [pltpu.VMEM((groups, PACK, OWN), BF16)] * 2
    lagged = pl.pallas_call(
        functools.partial(filter_kernel, groups, inner),
        out_shape=pltpu.VMEM((3 * OWN * LAGS, OWN), F32),
        in_specs=[far] * len(operands),
        out_specs=pl.BlockSpec(memory_space=pltpu.VMEM),
        scratch_shapes=[pltpu.VMEM(array.shape, array.dtype) for array in operands]
        + [pltpu.SemaphoreType.DMA((len(operands) + 1,))]
        + messages + [pltpu.SemaphoreType.DMA] * 4 + [pltpu.SemaphoreType.DMA((2,))] * 2
        + [
            pltpu.VMEM((OWN, 2 * BINS), BF16),
            pltpu.VMEM((2, OWN, 2 * BINS), BF16),
            pltpu.VMEM((2 * OWN, LENGTH), F32),
            pltpu.VMEM((PACK * (groups + 2), OWN), F32),
            pltpu.VMEM((3 * OWN, LENGTH), BF16),
            pltpu.VMEM((LAGS * OWN, LENGTH), BF16),
        ],
        compiler_params=pltpu.CompilerParams(
            collective_id=0, has_side_effects=True, vmem_limit_bytes=40 * 2**20
        ),
        name="fan_filter_products",
    )(*operands)
    lagged = pltpu.with_memory_space_constraint(lagged, pltpu.VMEM)
    return pl.pallas_call(
        write_kernel,
        out_shape=jax.ShapeDtypeStruct((OWN, BAND * LAGS), F32),
        in_specs=[pl.BlockSpec(memory_space=pltpu.VMEM)],
        out_specs=far,
        scratch_shapes=[pltpu.VMEM((OWN, BAND * LAGS), F32), pltpu.SemaphoreType.DMA],
        compiler_params=pltpu.CompilerParams(vmem_limit_bytes=20 * 2**20),
        name="correlation_rows",
    )(lagged)


def solution(mesh):
    groups, inner = mesh.size, mesh.shape["cy"]
    return jax.shard_map(
        functools.partial(body, groups, inner),
        mesh=mesh,
        in_specs=(P(("cx", "cy"), None), P()),
        out_specs=P(("cx", "cy"), None),
        check_vma=False,
    )
```

```python
import functools
import itertools
import math

import jax
import jax.numpy as jnp
import numpy as np
from jax import lax
from jax.experimental import pallas as pl
from jax.experimental.pallas import tpu as pltpu
from jax.sharding import PartitionSpec as P

BAND = 256
LAGS = 16
BINS = 256
OWN = 128
LENGTH = 1024
MESH = pl.DeviceIdType.MESH
F32 = jnp.float32
BF16 = jnp.bfloat16


def halves(table):
    high = table.astype(BF16)
    return high, (table - high.astype(np.float64)).astype(BF16)


def tables(groups):
    bin_index = np.arange(BINS, dtype=np.int64)
    angle = 2.0 * math.pi / LENGTH * (bin_index[:, None] * np.arange(LENGTH)[None, :] % LENGTH)
    pairs = np.stack([np.cos(angle), -np.sin(angle)], axis=1).reshape(groups, 2, 2, LENGTH)
    time = pairs.transpose(2, 1, 0, 3).reshape(2 * BINS, LENGTH)
    time[2 * groups] = np.cos(math.pi * np.arange(LENGTH))
    angle = 2.0 * math.pi / LENGTH * ((bin_index + BINS)[:, None] * np.arange(LENGTH)[None, :] % LENGTH)
    upper = np.concatenate([np.cos(angle), -np.sin(angle)])
    index = np.arange(groups)
    angle = 2.0 * math.pi / groups * (index[:, None] * index[None, :] % groups)
    re, im = np.cos(angle), -np.sin(angle)
    wide = np.block([[re, -im], [im, re]])
    angle = 2.0 * math.pi / (groups * OWN) * (index[:, None] * index[None, :])
    twist = np.stack([np.cos(angle), np.sin(angle)]).astype(np.float32)
    return np.stack(halves(time)), np.stack([*halves(wide), *halves(wide.T)]), twist, np.stack(halves(upper))


def dot(left, right, dims=((1,), (0,))):
    return lax.dot_general(left, right, (dims, ((), ())), preferred_element_type=F32)


def split(value):
    high = value.astype(BF16)
    return high, (value - high.astype(F32)).astype(BF16)


def dot_three(left, right):
    return dot(left[0], right[0]) + (dot(left[0], right[1]) + dot(left[1], right[0]))


def blocks(value):
    return value[:OWN, :OWN], value[:OWN, OWN:], value[OWN:, :OWN], value[OWN:, OWN:]


def join(a, b, c, d):
    return jnp.concatenate([jnp.concatenate([a, b], axis=1), jnp.concatenate([c, d], axis=1)], axis=0)


def least_cut(cut):
    row = lax.broadcasted_iota(jnp.int32, (OWN, OWN), 0)
    col = lax.broadcasted_iota(jnp.int32, (OWN, OWN), 1)
    mirror = (((row + col) % OWN) == 0).astype(F32).astype(BF16)
    reverse = ((row + col) == OWN - 1).astype(F32).astype(BF16)
    exact = cut.astype(F32).astype(BF16)
    across = dot(exact, mirror).astype(BF16)
    mirrored = jnp.where(col == 0, dot(mirror, across), dot(reverse, across))
    return jnp.maximum(cut.astype(F32), mirrored).T


TILES = BAND * LAGS // OWN
TILE_ROWS = OWN // 8
PACK = 16


def finish(lagged, out, first, last):
    lane = lax.broadcasted_iota(jnp.int32, (8, OWN), 1)
    odd = [(lane // step) % 2 == 1 for step in (1, 2, 4)]
    known = {}

    def skewed(bit, spot):
        if (bit, spot) not in known:
            known[bit, spot] = lagged[pl.ds(8 * spot, 8), :] if bit == 0 else jnp.where(
                odd[bit - 1], skewed(bit - 1, spot + (1 << bit)), skewed(bit - 1, spot)
            )
        return known[bit, spot]

    for tile in range(first, last):
        turned = jnp.concatenate([skewed(3, tile * TILE_ROWS + number) for number in range(TILE_ROWS)], axis=0).T
        for group in range(max(0, tile - TILES + 1), min(TILE_ROWS, tile + 1)):
            out[pl.ds(8 * group, 8), pl.ds((tile - group) * OWN, OWN)] = turned[8 * group:8 * group + 8]


def filter_kernel(
    groups, inner,
    signal_far, cut_far, time_far, wide_far, twist_far, upper_far,
    lagged,
    signal, cut, time, wide_all, twist, upper, load_sems,
    out_first, in_first, out_second, in_second,
    send_first, recv_first, send_second, recv_second, send_upper, recv_upper,
    upper_out, upper_in, upper_sides, packed, ext, lags,
):
    outer_at, inner_at = lax.axis_index("cx"), lax.axis_index("cy")
    me = outer_at * inner + inner_at

    def at(device):
        return (device // inner, device % inner)

    def peer(step):
        return lax.rem(me + step, groups)

    def visit_others(visit):
        high, mid, core = outer_at // 8, lax.rem(outer_at // 2, 4), lax.rem(outer_at, 2)
        top, low = inner_at // 4, lax.rem(inner_at, 4)
        highs, cores, tops = (8 * high, 8 - 8 * high), (core, 1 - core), (4 * top, 4 - 4 * top)
        mids = [2 * lax.rem(mid + step, 4) for step in range(4)]
        lows = [lax.rem(low + step, 4) for step in range(4)]
        ring = (0, 1, 2, 1)
        offsets = sorted(
            itertools.product(range(4), range(4), range(2), range(2), range(2)),
            key=lambda o: (-(ring[o[0]] + ring[o[1]] + 2 * o[2] + o[3]),
                           (o[0] * 7 + o[1] * 5 + o[2] * 3 + o[3] * 11 + o[4] * 13) % 17),
        )
        for mid_step, low_step, flip_top, flip_high, flip_core in offsets:
            if mid_step + low_step + flip_top + flip_high + flip_core > 0:
                visit(highs[flip_high] + mids[mid_step] + cores[flip_core], tops[flip_top] + lows[low_step])

    pairs = ((signal_far, signal), (time_far.at[0], time.at[0]), (time_far.at[1], time.at[1]),
             (cut_far, cut), (wide_far, wide_all), (twist_far, twist), (upper_far, upper))
    loads = [pltpu.make_async_copy(far, near, load_sems.at[number]) for number, (far, near) in enumerate(pairs)]
    for load in loads[:-1]:
        load.start()

    barrier = pltpu.get_barrier_semaphore()

    def greet(cx, cy):
        pl.semaphore_signal(barrier, inc=1, device_id=(cx, cy), device_id_type=MESH)

    visit_others(greet)
    loads[0].wait()
    time_high, time_low = time.at[0], time.at[1]
    own_high, own_low = split(signal[...])
    both = jnp.concatenate([own_high, own_low], axis=0)
    loads[1].wait()
    wide_sum = dot(time_high[...], both, ((1,), (1,)))
    loads[2].wait()
    spectrum = (wide_sum[:, :OWN] + wide_sum[:, OWN:]) + dot(time_low[...], own_high, ((1,), (1,)))
    for part in range(4):
        out_first[:, part, :] = spectrum[part * OWN:(part + 1) * OWN]

    loads[-1].start()
    pl.semaphore_wait(barrier, groups - 1)

    def exchange(outgoing, incoming, send_sem, recv_sem):
        def push(cx, cy):
            pltpu.make_async_remote_copy(
                src_ref=outgoing.at[cx * inner + cy],
                dst_ref=incoming.at[me],
                send_sem=send_sem,
                recv_sem=recv_sem,
                device_id=(cx, cy),
                device_id_type=MESH,
            ).start()

        visit_others(push)
        incoming[me] = outgoing[me]

    def settle(outgoing, incoming, send_sem, recv_sem):
        rest = pltpu.make_async_remote_copy(
            src_ref=outgoing.at[pl.ds(0, groups - 1)],
            dst_ref=incoming.at[pl.ds(0, groups - 1)],
            send_sem=send_sem,
            recv_sem=recv_sem,
            device_id=at(peer(1)),
            device_id_type=MESH,
        )
        rest.wait()

    exchange(out_first, in_first, send_first, recv_first)
    for load in loads[3:]:
        load.wait()
    upper_sum = dot(both, upper[0], ((1,), (1,)))
    upper_sum = (upper_sum[:OWN] + upper_sum[OWN:]) + dot(own_high, upper[1], ((1,), (1,)))
    upper_out[...] = (upper_sum * (2.0 / LENGTH)).astype(BF16)

    early = [
        pltpu.make_async_remote_copy(
            src_ref=upper_out, dst_ref=upper_in.at[side],
            send_sem=send_upper.at[side], recv_sem=recv_upper.at[side],
            device_id=at(peer(1 if side == 0 else groups - 1)), device_id_type=MESH,
        )
        for side in range(2)
    ]
    for copy in early:
        copy.start()
    cut_least = least_cut(cut[...])
    wide = (wide_all[0], wide_all[1])
    flip = (wide_all[2], wide_all[3])
    cosine, sine = twist[0], twist[1]
    settle(out_first, in_first, send_first, recv_first)

    rows = [in_first[:, part, :] for part in range(4)]
    value = dot_three(wide, split(join(rows[0], rows[1], rows[2] * jnp.where(me == 0, 0.0, 1.0), rows[3])))
    re_a, re_b, im_a, im_b = blocks(value)
    value = join(
        re_a * cosine + im_a * sine, im_a * cosine - re_a * sine,
        re_b * cosine + im_b * sine, im_b * cosine - re_b * sine,
    )
    value = dot_three(split(value), flip)
    even = (2 * me).astype(F32)
    scale = -2.0 / (LENGTH * groups * OWN)
    keep_a = jnp.where(cut_least > even, jnp.where(me == 0, 0.5 * scale, scale), 0.0)
    keep_b = jnp.where(cut_least > even + 1.0, scale, 0.0)
    value = value * join(keep_a, keep_a, keep_b, keep_b)
    value = dot_three(split(value), wide)
    re_a, im_a, re_b, im_b = blocks(value)
    value = join(
        re_a * cosine - im_a * sine, re_b * cosine - im_b * sine,
        im_a * cosine + re_a * sine, im_b * cosine + re_b * sine,
    )
    value = dot_three(flip, split(value))
    for part, block in enumerate(blocks(value)):
        weight = 2.0 / LENGTH if part % 2 else jnp.where(me == 0, 1.0 / LENGTH, 2.0 / LENGTH)
        kept = rows[part] * weight + block
        for first, array in (
            (PACK, block), (PACK + 4, block - block.astype(BF16).astype(F32)), (2 * PACK + 8, kept), (12, kept),
        ):
            packed[pl.ds(first + part, groups, stride=PACK), :] = array
    for first in (PACK + 8, PACK * groups + 12):
        packed[pl.ds(first, 4), :] = jnp.zeros((4, OWN), F32)
    out_second[...] = packed[pl.ds(PACK, PACK * groups), :].astype(BF16).reshape(groups, PACK, OWN)

    exchange(out_second, in_second, send_second, recv_second)
    for copy in early:
        copy.wait_recv()
    bins = upper_in[...].reshape(2 * OWN, 2 * BINS)
    row = lax.broadcasted_iota(jnp.int32, (2 * OWN, LENGTH), 0)
    inside = jnp.where(row < OWN, (me > 0).astype(F32), (me < groups - 1).astype(F32))
    upper_sides[...] = (dot(bins, upper[0]) + dot(bins, upper[1])) * inside
    settle(out_second, in_second, send_second, recv_second)

    packed[pl.ds(0, PACK * groups), :] = in_second[...].astype(F32).reshape(PACK * groups, OWN)

    def turn(*firsts):
        parts = [[packed[pl.ds(first + part, groups, stride=PACK), :] for first in firsts] for part in range(4)]
        return jnp.concatenate([sum(part[1:], part[0]).T for part in parts], axis=1)

    back_high, back_low = split(turn(0, 4))
    all_bins = jnp.concatenate([back_high, back_low, turn(8).astype(BF16), turn(12).astype(BF16)], axis=0)
    chunk = 256
    for number in range(LENGTH // chunk):
        span = pl.ds(number * chunk, chunk)
        sums = dot(all_bins, time_high[:, span])
        rejected = (sums[:OWN] + sums[OWN:2 * OWN]) + dot(back_high, time_low[:, span])
        ext[pl.ds(OWN, OWN), span] = (signal[:, span] + rejected).astype(BF16)
        ext[pl.ds(0, OWN), span] = (upper_sides[pl.ds(0, OWN), span] + sums[2 * OWN:3 * OWN]).astype(BF16)
        ext[pl.ds(2 * OWN, OWN), span] = (upper_sides[pl.ds(OWN, OWN), span] + sums[3 * OWN:]).astype(BF16)
    own = ext[pl.ds(OWN, OWN), :] * jnp.asarray(1.0 / math.sqrt(LENGTH), BF16)
    for lag in range(LAGS):
        lags[pl.ds(lag * OWN, OWN), :] = own if lag == 0 else jnp.concatenate(
            [jnp.zeros((OWN, lag), BF16), own[:, :LENGTH - lag]], axis=1
        )

    everything = ext[...]
    for number in range(LAGS // 2):
        values = dot(everything, lags[pl.ds(number * 2 * OWN, 2 * OWN), :], ((1,), (1,)))
        for side in range(2):
            lagged[pl.ds(2 * number + side, 3 * OWN, stride=LAGS), :] = values[:, side * OWN:(side + 1) * OWN]
    for copy in early:
        copy.wait_send()


def write_kernel(lagged, out_far, out, store_sem):
    done = 0
    for last in range(TILE_ROWS + TILES // 4 - 1, TILE_ROWS + TILES, TILES // 4):
        finish(lagged, out, done, last)
        done = last
        columns = pl.ds((last - TILE_ROWS + 1 - TILES // 4) * OWN, TILES // 4 * OWN)
        pltpu.make_async_copy(out.at[:, columns], out_far.at[:, columns], store_sem).start()
    pltpu.make_async_copy(out, out_far, store_sem).wait()


def body(groups, inner, signal, fan_cut):
    operands = [signal, fan_cut.reshape(OWN, groups), *(jnp.asarray(table) for table in tables(groups))]
    operands = [pltpu.with_memory_space_constraint(array, pltpu.HBM) for array in operands]
    far = pl.BlockSpec(memory_space=pltpu.HBM)
    messages = [pltpu.VMEM((groups, 4, OWN), F32)] * 2 + [pltpu.VMEM((groups, PACK, OWN), BF16)] * 2
    lagged = pl.pallas_call(
        functools.partial(filter_kernel, groups, inner),
        out_shape=pltpu.VMEM((3 * OWN * LAGS, OWN), F32),
        in_specs=[far] * len(operands),
        out_specs=pl.BlockSpec(memory_space=pltpu.VMEM),
        scratch_shapes=[pltpu.VMEM(array.shape, array.dtype) for array in operands]
        + [pltpu.SemaphoreType.DMA((len(operands) + 1,))]
        + messages + [pltpu.SemaphoreType.DMA] * 4 + [pltpu.SemaphoreType.DMA((2,))] * 2
        + [
            pltpu.VMEM((OWN, 2 * BINS), BF16),
            pltpu.VMEM((2, OWN, 2 * BINS), BF16),
            pltpu.VMEM((2 * OWN, LENGTH), F32),
            pltpu.VMEM((PACK * (groups + 2), OWN), F32),
            pltpu.VMEM((3 * OWN, LENGTH), BF16),
            pltpu.VMEM((LAGS * OWN, LENGTH), BF16),
        ],
        compiler_params=pltpu.CompilerParams(
            collective_id=0, has_side_effects=True, vmem_limit_bytes=40 * 2**20
        ),
        name="fan_filter_products",
    )(*operands)
    lagged = pltpu.with_memory_space_constraint(lagged, pltpu.VMEM)
    return pl.pallas_call(
        write_kernel,
        out_shape=jax.ShapeDtypeStruct((OWN, BAND * LAGS), F32),
        in_specs=[pl.BlockSpec(memory_space=pltpu.VMEM)],
        out_specs=far,
        scratch_shapes=[pltpu.VMEM((OWN, BAND * LAGS), F32), pltpu.SemaphoreType.DMA],
        compiler_params=pltpu.CompilerParams(vmem_limit_bytes=20 * 2**20),
        name="correlation_rows",
    )(lagged)


def solution(mesh):
    groups, inner = mesh.size, mesh.shape["cy"]
    return jax.shard_map(
        functools.partial(body, groups, inner),
        mesh=mesh,
        in_specs=(P(("cx", "cy"), None), P()),
        out_specs=P(("cx", "cy"), None),
        check_vma=False,
    )
```

```python
import functools
import itertools
import math

import jax
import jax.numpy as jnp
import numpy as np
from jax import lax
from jax.experimental import pallas as pl
from jax.experimental.pallas import tpu as pltpu
from jax.sharding import PartitionSpec as P

BAND = 256
LAGS = 16
BINS = 256
OWN = 128
LENGTH = 1024
MESH = pl.DeviceIdType.MESH
F32 = jnp.float32
BF16 = jnp.bfloat16


def halves(table):
    high = table.astype(BF16)
    return high, (table - high.astype(np.float64)).astype(BF16)


def tables(groups):
    bin_index = np.arange(BINS, dtype=np.int64)
    angle = 2.0 * math.pi / LENGTH * (bin_index[:, None] * np.arange(LENGTH)[None, :] % LENGTH)
    pairs = np.stack([np.cos(angle), -np.sin(angle)], axis=1).reshape(groups, 2, 2, LENGTH)
    time = pairs.transpose(2, 1, 0, 3).reshape(2 * BINS, LENGTH)
    time[2 * groups] = np.cos(math.pi * np.arange(LENGTH))
    angle = 2.0 * math.pi / LENGTH * ((bin_index + BINS)[:, None] * np.arange(LENGTH)[None, :] % LENGTH)
    upper = np.concatenate([np.cos(angle), -np.sin(angle)])
    index = np.arange(groups)
    angle = 2.0 * math.pi / groups * (index[:, None] * index[None, :] % groups)
    re, im = np.cos(angle), -np.sin(angle)
    wide = np.block([[re, -im], [im, re]])
    angle = 2.0 * math.pi / (groups * OWN) * (index[:, None] * index[None, :])
    twist = np.stack([np.cos(angle), np.sin(angle)]).astype(np.float32)
    return np.stack(halves(time)), np.stack([*halves(wide), *halves(wide.T)]), twist, np.stack(halves(upper))


def dot(left, right, dims=((1,), (0,))):
    return lax.dot_general(left, right, (dims, ((), ())), preferred_element_type=F32)


def split(value):
    high = value.astype(BF16)
    return high, (value - high.astype(F32)).astype(BF16)


def dot_three(left, right):
    return dot(left[0], right[0]) + (dot(left[0], right[1]) + dot(left[1], right[0]))


def least_cut(cut):
    row = lax.broadcasted_iota(jnp.int32, (OWN, OWN), 0)
    col = lax.broadcasted_iota(jnp.int32, (OWN, OWN), 1)
    mirror = (((row + col) % OWN) == 0).astype(F32).astype(BF16)
    reverse = ((row + col) == OWN - 1).astype(F32).astype(BF16)
    exact = cut.astype(F32).astype(BF16)
    across = dot(exact, mirror).astype(BF16)
    mirrored = jnp.where(col == 0, dot(mirror, across), dot(reverse, across))
    return jnp.maximum(cut.astype(F32), mirrored).T


TILES = BAND * LAGS // OWN
TILE_ROWS = OWN // 8
PACK = 16


def finish(lagged, out, first, last):
    lane = lax.broadcasted_iota(jnp.int32, (8, OWN), 1)
    odd = [(lane // step) % 2 == 1 for step in (1, 2, 4)]
    known = {}

    def skewed(bit, spot):
        if (bit, spot) not in known:
            known[bit, spot] = lagged[pl.ds(8 * spot, 8), :] if bit == 0 else jnp.where(
                odd[bit - 1], skewed(bit - 1, spot + (1 << bit)), skewed(bit - 1, spot)
            )
        return known[bit, spot]

    for tile in range(first, last):
        turned = jnp.concatenate([skewed(3, tile * TILE_ROWS + number) for number in range(TILE_ROWS)], axis=0).T
        for group in range(max(0, tile - TILES + 1), min(TILE_ROWS, tile + 1)):
            out[pl.ds(8 * group, 8), pl.ds((tile - group) * OWN, OWN)] = turned[8 * group:8 * group + 8]


def filter_kernel(
    groups, inner,
    signal_far, cut_far, time_far, wide_far, twist_far, upper_far,
    lagged,
    signal, cut, time, wide_all, twist, upper, load_sems,
    out_first, in_first, out_second, in_second,
    send_first, recv_first, send_second, recv_second, send_upper, recv_upper,
    upper_out, upper_in, upper_sides, packed, ext, lags,
):
    outer_at, inner_at = lax.axis_index("cx"), lax.axis_index("cy")
    me = outer_at * inner + inner_at

    def at(device):
        return (device // inner, device % inner)

    def peer(step):
        return lax.rem(me + step, groups)

    def visit_others(visit):
        high, mid, core = outer_at // 8, lax.rem(outer_at // 2, 4), lax.rem(outer_at, 2)
        top, low = inner_at // 4, lax.rem(inner_at, 4)
        highs, cores, tops = (8 * high, 8 - 8 * high), (core, 1 - core), (4 * top, 4 - 4 * top)
        mids = [2 * lax.rem(mid + step, 4) for step in range(4)]
        lows = [lax.rem(low + step, 4) for step in range(4)]
        ring = (0, 1, 2, 1)
        offsets = sorted(
            itertools.product(range(4), range(4), range(2), range(2), range(2)),
            key=lambda o: (-(ring[o[0]] + ring[o[1]] + 2 * o[2] + o[3]),
                           (o[0] * 7 + o[1] * 5 + o[2] * 3 + o[3] * 11 + o[4] * 13) % 17),
        )
        for mid_step, low_step, flip_top, flip_high, flip_core in offsets:
            if mid_step + low_step + flip_top + flip_high + flip_core > 0:
                visit(highs[flip_high] + mids[mid_step] + cores[flip_core], tops[flip_top] + lows[low_step])

    pairs = ((signal_far, signal), (time_far.at[0], time.at[0]), (time_far.at[1], time.at[1]),
             (cut_far, cut), (wide_far, wide_all), (twist_far, twist), (upper_far, upper))
    loads = [pltpu.make_async_copy(far, near, load_sems.at[number]) for number, (far, near) in enumerate(pairs)]
    for load in loads[:-1]:
        load.start()

    barrier = pltpu.get_barrier_semaphore()

    def greet(cx, cy):
        pl.semaphore_signal(barrier, inc=1, device_id=(cx, cy), device_id_type=MESH)

    visit_others(greet)
    loads[0].wait()
    time_high, time_low = time.at[0], time.at[1]
    own_high, own_low = split(signal[...])
    both = jnp.concatenate([own_high, own_low], axis=0)
    loads[1].wait()
    wide_sum = dot(time_high[...], both, ((1,), (1,)))
    loads[2].wait()
    spectrum = (wide_sum[:, :OWN] + wide_sum[:, OWN:]) + dot(time_low[...], own_high, ((1,), (1,)))
    for part in range(4):
        out_first[:, part, :] = spectrum[part * OWN:(part + 1) * OWN]

    loads[-1].start()
    pl.semaphore_wait(barrier, groups - 1)

    def exchange(outgoing, incoming, send_sem, recv_sem):
        def push(cx, cy):
            pltpu.make_async_remote_copy(
                src_ref=outgoing.at[cx * inner + cy],
                dst_ref=incoming.at[me],
                send_sem=send_sem,
                recv_sem=recv_sem,
                device_id=(cx, cy),
                device_id_type=MESH,
            ).start()

        visit_others(push)
        incoming[me] = outgoing[me]

    def settle(outgoing, incoming, send_sem, recv_sem):
        rest = pltpu.make_async_remote_copy(
            src_ref=outgoing.at[pl.ds(0, groups - 1)],
            dst_ref=incoming.at[pl.ds(0, groups - 1)],
            send_sem=send_sem,
            recv_sem=recv_sem,
            device_id=at(peer(1)),
            device_id_type=MESH,
        )
        rest.wait()

    exchange(out_first, in_first, send_first, recv_first)
    for load in loads[3:]:
        load.wait()
    upper_sum = dot(both, upper[0], ((1,), (1,)))
    upper_sum = (upper_sum[:OWN] + upper_sum[OWN:]) + dot(own_high, upper[1], ((1,), (1,)))
    upper_out[...] = (upper_sum * (2.0 / LENGTH)).astype(BF16)

    early = [
        pltpu.make_async_remote_copy(
            src_ref=upper_out, dst_ref=upper_in.at[side],
            send_sem=send_upper.at[side], recv_sem=recv_upper.at[side],
            device_id=at(peer(1 if side == 0 else groups - 1)), device_id_type=MESH,
        )
        for side in range(2)
    ]
    for copy in early:
        copy.start()
    cut_least = least_cut(cut[...])
    wide = (wide_all[0], wide_all[1])
    flip = (wide_all[2], wide_all[3])
    cosine, sine = twist[0], twist[1]
    settle(out_first, in_first, send_first, recv_first)

    rows = [in_first[:, part, :] for part in range(4)]
    real_zero = rows[2] * jnp.where(me == 0, 0.0, 1.0)
    values = [jnp.concatenate(pair, axis=0) for pair in ((rows[0], real_zero), (rows[1], rows[3]))]
    values = [dot_three(wide, split(value)) for value in values]
    values = [
        jnp.concatenate([re * cosine + im * sine, im * cosine - re * sine], axis=1)
        for re, im in ((value[:OWN], value[OWN:]) for value in values)
    ]
    values = [dot_three(split(value), flip) for value in values]
    even = (2 * me).astype(F32)
    scale = -2.0 / (LENGTH * groups * OWN)
    rejects = (
        jnp.where(cut_least > even, jnp.where(me == 0, 0.5 * scale, scale), 0.0),
        jnp.where(cut_least > even + 1.0, scale, 0.0),
    )
    values = [value * jnp.concatenate([reject, reject], axis=1) for value, reject in zip(values, rejects)]
    values = [dot_three(split(value), wide) for value in values]
    values = [
        jnp.concatenate([re * cosine - im * sine, im * cosine + re * sine], axis=0)
        for re, im in ((value[:, :OWN], value[:, OWN:]) for value in values)
    ]
    values = [dot_three(flip, split(value)) for value in values]
    for part in range(4):
        block = values[part % 2][(part // 2) * OWN:(part // 2 + 1) * OWN]
        weight = 2.0 / LENGTH if part % 2 else jnp.where(me == 0, 1.0 / LENGTH, 2.0 / LENGTH)
        kept = rows[part] * weight + block
        for first, array in (
            (PACK, block), (PACK + 4, block - block.astype(BF16).astype(F32)), (2 * PACK + 8, kept), (12, kept),
        ):
            packed[pl.ds(first + part, groups, stride=PACK), :] = array
    for first in (PACK + 8, PACK * groups + 12):
        packed[pl.ds(first, 4), :] = jnp.zeros((4, OWN), F32)
    out_second[...] = packed[pl.ds(PACK, PACK * groups), :].astype(BF16).reshape(groups, PACK, OWN)

    exchange(out_second, in_second, send_second, recv_second)
    for copy in early:
        copy.wait_recv()
    bins = upper_in[...].reshape(2 * OWN, 2 * BINS)
    row = lax.broadcasted_iota(jnp.int32, (2 * OWN, LENGTH), 0)
    inside = jnp.where(row < OWN, (me > 0).astype(F32), (me < groups - 1).astype(F32))
    upper_sides[...] = (dot(bins, upper[0]) + dot(bins, upper[1])) * inside
    settle(out_second, in_second, send_second, recv_second)

    packed[pl.ds(0, PACK * groups), :] = in_second[...].astype(F32).reshape(PACK * groups, OWN)

    def turn(*firsts):
        parts = [[packed[pl.ds(first + part, groups, stride=PACK), :] for first in firsts] for part in range(4)]
        return jnp.concatenate([sum(part[1:], part[0]).T for part in parts], axis=1)

    back_high, back_low = split(turn(0, 4))
    all_bins = jnp.concatenate([back_high, back_low, turn(8).astype(BF16), turn(12).astype(BF16)], axis=0)
    chunk = 256
    for number in range(LENGTH // chunk):
        span = pl.ds(number * chunk, chunk)
        sums = dot(all_bins, time_high[:, span])
        rejected = (sums[:OWN] + sums[OWN:2 * OWN]) + dot(back_high, time_low[:, span])
        ext[pl.ds(OWN, OWN), span] = (signal[:, span] + rejected).astype(BF16)
        ext[pl.ds(0, OWN), span] = (upper_sides[pl.ds(0, OWN), span] + sums[2 * OWN:3 * OWN]).astype(BF16)
        ext[pl.ds(2 * OWN, OWN), span] = (upper_sides[pl.ds(OWN, OWN), span] + sums[3 * OWN:]).astype(BF16)
    own = ext[pl.ds(OWN, OWN), :] * jnp.asarray(1.0 / math.sqrt(LENGTH), BF16)
    for lag in range(LAGS):
        lags[pl.ds(lag * OWN, OWN), :] = own if lag == 0 else jnp.concatenate(
            [jnp.zeros((OWN, lag), BF16), own[:, :LENGTH - lag]], axis=1
        )

    everything = ext[...]
    for number in range(LAGS // 2):
        values = dot(everything, lags[pl.ds(number * 2 * OWN, 2 * OWN), :], ((1,), (1,)))
        for side in range(2):
            lagged[pl.ds(2 * number + side, 3 * OWN, stride=LAGS), :] = values[:, side * OWN:(side + 1) * OWN]
    for copy in early:
        copy.wait_send()


def write_kernel(lagged, out_far, out, store_sem):
    done = 0
    for last in range(TILE_ROWS + TILES // 4 - 1, TILE_ROWS + TILES, TILES // 4):
        finish(lagged, out, done, last)
        done = last
        columns = pl.ds((last - TILE_ROWS + 1 - TILES // 4) * OWN, TILES // 4 * OWN)
        pltpu.make_async_copy(out.at[:, columns], out_far.at[:, columns], store_sem).start()
    pltpu.make_async_copy(out, out_far, store_sem).wait()


def body(groups, inner, signal, fan_cut):
    operands = [signal, fan_cut.reshape(OWN, groups), *(jnp.asarray(table) for table in tables(groups))]
    operands = [pltpu.with_memory_space_constraint(array, pltpu.HBM) for array in operands]
    far = pl.BlockSpec(memory_space=pltpu.HBM)
    messages = [pltpu.VMEM((groups, 4, OWN), F32)] * 2 + [pltpu.VMEM((groups, PACK, OWN), BF16)] * 2
    lagged = pl.pallas_call(
        functools.partial(filter_kernel, groups, inner),
        out_shape=pltpu.VMEM(((3 * OWN + 1) * LAGS, OWN), F32),
        in_specs=[far] * len(operands),
        out_specs=pl.BlockSpec(memory_space=pltpu.VMEM),
        scratch_shapes=[pltpu.VMEM(array.shape, array.dtype) for array in operands]
        + [pltpu.SemaphoreType.DMA((len(operands) + 1,))]
        + messages + [pltpu.SemaphoreType.DMA] * 4 + [pltpu.SemaphoreType.DMA((2,))] * 2
        + [
            pltpu.VMEM((OWN, 2 * BINS), BF16),
            pltpu.VMEM((2, OWN, 2 * BINS), BF16),
            pltpu.VMEM((2 * OWN, LENGTH), F32),
            pltpu.VMEM((PACK * (groups + 4), OWN), F32),
            pltpu.VMEM((3 * OWN, LENGTH), BF16),
            pltpu.VMEM((LAGS * OWN, LENGTH), BF16),
        ],
        compiler_params=pltpu.CompilerParams(
            collective_id=0, has_side_effects=True, vmem_limit_bytes=40 * 2**20
        ),
        name="fan_filter_products",
    )(*operands)
    lagged = pltpu.with_memory_space_constraint(lagged, pltpu.VMEM)
    return pl.pallas_call(
        write_kernel,
        out_shape=jax.ShapeDtypeStruct((OWN, BAND * LAGS), F32),
        in_specs=[pl.BlockSpec(memory_space=pltpu.VMEM)],
        out_specs=far,
        scratch_shapes=[pltpu.VMEM((OWN, BAND * LAGS), F32), pltpu.SemaphoreType.DMA],
        compiler_params=pltpu.CompilerParams(vmem_limit_bytes=20 * 2**20),
        name="correlation_rows",
    )(lagged)


def solution(mesh):
    groups, inner = mesh.size, mesh.shape["cy"]
    return jax.shard_map(
        functools.partial(body, groups, inner),
        mesh=mesh,
        in_specs=(P(("cx", "cy"), None), P()),
        out_specs=P(("cx", "cy"), None),
        check_vma=False,
    )
```

```python
import functools
import itertools
import math

import jax
import jax.numpy as jnp
import numpy as np
from jax import lax
from jax.experimental import pallas as pl
from jax.experimental.pallas import tpu as pltpu
from jax.sharding import PartitionSpec as P

BAND = 256
LAGS = 16
BINS = 256
OWN = 128
LENGTH = 1024
MESH = pl.DeviceIdType.MESH
F32 = jnp.float32
BF16 = jnp.bfloat16


def halves(table):
    high = table.astype(BF16)
    return high, (table - high.astype(np.float64)).astype(BF16)


def tables(groups):
    bin_index = np.arange(BINS, dtype=np.int64)
    angle = 2.0 * math.pi / LENGTH * (bin_index[:, None] * np.arange(LENGTH)[None, :] % LENGTH)
    pairs = np.stack([np.cos(angle), -np.sin(angle)], axis=1).reshape(groups, 2, 2, LENGTH)
    time = pairs.transpose(2, 1, 0, 3).reshape(2 * BINS, LENGTH)
    time[2 * groups] = np.cos(math.pi * np.arange(LENGTH))
    angle = 2.0 * math.pi / LENGTH * ((bin_index + BINS)[:, None] * np.arange(LENGTH)[None, :] % LENGTH)
    upper = np.concatenate([np.cos(angle), -np.sin(angle)])
    index = np.arange(groups)
    angle = 2.0 * math.pi / groups * (index[:, None] * index[None, :] % groups)
    re, im = np.cos(angle), -np.sin(angle)
    wide = np.block([[re, -im], [im, re]])
    angle = 2.0 * math.pi / (groups * OWN) * (index[:, None] * index[None, :])
    twist = np.stack([np.cos(angle), np.sin(angle)]).astype(np.float32)
    return np.stack(halves(time)), np.stack([*halves(wide), *halves(wide.T)]), twist, np.stack(halves(upper))


def dot(left, right, dims=((1,), (0,))):
    return lax.dot_general(left, right, (dims, ((), ())), preferred_element_type=F32)


def split(value):
    high = value.astype(BF16)
    return high, (value - high.astype(F32)).astype(BF16)


def dot_three(left, right):
    return dot(left[0], right[0]) + (dot(left[0], right[1]) + dot(left[1], right[0]))


def least_cut(cut):
    row = lax.broadcasted_iota(jnp.int32, (OWN, OWN), 0)
    col = lax.broadcasted_iota(jnp.int32, (OWN, OWN), 1)
    mirror = (((row + col) % OWN) == 0).astype(F32).astype(BF16)
    reverse = ((row + col) == OWN - 1).astype(F32).astype(BF16)
    exact = cut.astype(F32).astype(BF16)
    across = dot(exact, mirror).astype(BF16)
    mirrored = jnp.where(col == 0, dot(mirror, across), dot(reverse, across))
    return jnp.maximum(cut.astype(F32), mirrored).T


TILES = BAND * LAGS // OWN
TILE_ROWS = OWN // 8
PACK = 16


def finish(lagged, out, first, last):
    lane = lax.broadcasted_iota(jnp.int32, (8, OWN), 1)
    odd = [(lane // step) % 2 == 1 for step in (1, 2, 4)]
    odd_lag = lax.broadcasted_iota(jnp.int32, (OWN, OWN), 1) % 2 == 1
    known = {}

    def skewed(bit, spot):
        if (bit, spot) not in known:
            known[bit, spot] = lagged[pl.ds(8 * spot, 8), :] if bit == 0 else jnp.where(
                odd[bit - 1], skewed(bit - 1, spot + (1 << bit)), skewed(bit - 1, spot)
            )
        return known[bit, spot]

    for tile in range(first, last):
        turned = jnp.concatenate([skewed(3, tile * TILE_ROWS + number) for number in range(TILE_ROWS)], axis=0).T
        swapped = jnp.concatenate([turned[OWN // 2:], turned[:OWN // 2]], axis=0)
        turned = jnp.where(odd_lag, swapped, turned)
        for group in range(max(0, tile - TILES + 1), min(TILE_ROWS, tile + 1)):
            out[pl.ds(8 * group, 8), pl.ds((tile - group) * OWN, OWN)] = turned[8 * group:8 * group + 8]


def filter_kernel(
    groups, inner,
    signal_far, cut_far, time_far, wide_far, twist_far, upper_far,
    lagged,
    signal, cut, time, wide_all, twist, upper, load_sems,
    out_first, in_first, out_second, in_second,
    send_first, recv_first, send_second, recv_second, send_upper, recv_upper,
    upper_out, upper_in, upper_sides, packed, ext, lags,
):
    outer_at, inner_at = lax.axis_index("cx"), lax.axis_index("cy")
    me = outer_at * inner + inner_at

    def at(device):
        return (device // inner, device % inner)

    def peer(step):
        return lax.rem(me + step, groups)

    def visit_others(visit):
        high, mid, core = outer_at // 8, lax.rem(outer_at // 2, 4), lax.rem(outer_at, 2)
        top, low = inner_at // 4, lax.rem(inner_at, 4)
        highs, cores, tops = (8 * high, 8 - 8 * high), (core, 1 - core), (4 * top, 4 - 4 * top)
        mids = [2 * lax.rem(mid + step, 4) for step in range(4)]
        lows = [lax.rem(low + step, 4) for step in range(4)]
        ring = (0, 1, 2, 1)
        offsets = sorted(
            itertools.product(range(4), range(4), range(2), range(2), range(2)),
            key=lambda o: (-(ring[o[0]] + ring[o[1]] + 2 * o[2] + o[3]),
                           (o[0] * 7 + o[1] * 5 + o[2] * 3 + o[3] * 11 + o[4] * 13) % 17),
        )
        for mid_step, low_step, flip_top, flip_high, flip_core in offsets:
            if mid_step + low_step + flip_top + flip_high + flip_core > 0:
                visit(highs[flip_high] + mids[mid_step] + cores[flip_core], tops[flip_top] + lows[low_step])

    pairs = ((signal_far, signal), (time_far.at[0], time.at[0]), (time_far.at[1], time.at[1]),
             (cut_far, cut), (wide_far, wide_all), (twist_far, twist), (upper_far, upper))
    loads = [pltpu.make_async_copy(far, near, load_sems.at[number]) for number, (far, near) in enumerate(pairs)]
    for load in loads[:-1]:
        load.start()

    barrier = pltpu.get_barrier_semaphore()

    def greet(cx, cy):
        pl.semaphore_signal(barrier, inc=1, device_id=(cx, cy), device_id_type=MESH)

    visit_others(greet)
    loads[0].wait()
    time_high, time_low = time.at[0], time.at[1]
    own_high, own_low = split(signal[...])
    both = jnp.concatenate([own_high, own_low], axis=0)
    loads[1].wait()
    wide_sum = dot(time_high[...], both, ((1,), (1,)))
    loads[2].wait()
    spectrum = (wide_sum[:, :OWN] + wide_sum[:, OWN:]) + dot(time_low[...], own_high, ((1,), (1,)))
    for part in range(4):
        out_first[:, part, :] = spectrum[part * OWN:(part + 1) * OWN]

    loads[-1].start()
    pl.semaphore_wait(barrier, groups - 1)

    def exchange(outgoing, incoming, send_sem, recv_sem):
        def push(cx, cy):
            pltpu.make_async_remote_copy(
                src_ref=outgoing.at[cx * inner + cy],
                dst_ref=incoming.at[me],
                send_sem=send_sem,
                recv_sem=recv_sem,
                device_id=(cx, cy),
                device_id_type=MESH,
            ).start()

        visit_others(push)
        incoming[me] = outgoing[me]

    def settle(outgoing, incoming, send_sem, recv_sem):
        rest = pltpu.make_async_remote_copy(
            src_ref=outgoing.at[pl.ds(0, groups - 1)],
            dst_ref=incoming.at[pl.ds(0, groups - 1)],
            send_sem=send_sem,
            recv_sem=recv_sem,
            device_id=at(peer(1)),
            device_id_type=MESH,
        )
        rest.wait()

    exchange(out_first, in_first, send_first, recv_first)
    for load in loads[3:]:
        load.wait()
    upper_sum = dot(both, upper[0], ((1,), (1,)))
    upper_sum = (upper_sum[:OWN] + upper_sum[OWN:]) + dot(own_high, upper[1], ((1,), (1,)))
    upper_out[...] = (upper_sum * (2.0 / LENGTH)).astype(BF16)

    early = [
        pltpu.make_async_remote_copy(
            src_ref=upper_out, dst_ref=upper_in.at[side],
            send_sem=send_upper.at[side], recv_sem=recv_upper.at[side],
            device_id=at(peer(1 if side == 0 else groups - 1)), device_id_type=MESH,
        )
        for side in range(2)
    ]
    for copy in early:
        copy.start()
    cut_least = least_cut(cut[...])
    wide = (wide_all[0], wide_all[1])
    flip = (wide_all[2], wide_all[3])
    cosine, sine = twist[0], twist[1]
    settle(out_first, in_first, send_first, recv_first)

    rows = [in_first[:, part, :] for part in range(4)]
    real_zero = rows[2] * jnp.where(me == 0, 0.0, 1.0)
    values = [jnp.concatenate(pair, axis=0) for pair in ((rows[0], real_zero), (rows[1], rows[3]))]
    values = [dot_three(wide, split(value)) for value in values]
    values = [
        jnp.concatenate([re * cosine + im * sine, im * cosine - re * sine], axis=1)
        for re, im in ((value[:OWN], value[OWN:]) for value in values)
    ]
    values = [dot_three(split(value), flip) for value in values]
    even = (2 * me).astype(F32)
    scale = -2.0 / (LENGTH * groups * OWN)
    rejects = (
        jnp.where(cut_least > even, jnp.where(me == 0, 0.5 * scale, scale), 0.0),
        jnp.where(cut_least > even + 1.0, scale, 0.0),
    )
    values = [value * jnp.concatenate([reject, reject], axis=1) for value, reject in zip(values, rejects)]
    values = [dot_three(split(value), wide) for value in values]
    values = [
        jnp.concatenate([re * cosine - im * sine, im * cosine + re * sine], axis=0)
        for re, im in ((value[:, :OWN], value[:, OWN:]) for value in values)
    ]
    values = [dot_three(flip, split(value)) for value in values]
    for part in range(4):
        block = values[part % 2][(part // 2) * OWN:(part // 2 + 1) * OWN]
        weight = 2.0 / LENGTH if part % 2 else jnp.where(me == 0, 1.0 / LENGTH, 2.0 / LENGTH)
        kept = rows[part] * weight + block
        for first, array in (
            (PACK, block), (PACK + 4, block - block.astype(BF16).astype(F32)), (2 * PACK + 8, kept), (12, kept),
        ):
            packed[pl.ds(first + part, groups, stride=PACK), :] = array
    for first in (PACK + 8, PACK * groups + 12):
        packed[pl.ds(first, 4), :] = jnp.zeros((4, OWN), F32)
    out_second[...] = packed[pl.ds(PACK, PACK * groups), :].astype(BF16).reshape(groups, PACK, OWN)

    exchange(out_second, in_second, send_second, recv_second)
    for copy in early:
        copy.wait_recv()
    bins = upper_in[...].reshape(2 * OWN, 2 * BINS)
    row = lax.broadcasted_iota(jnp.int32, (2 * OWN, LENGTH), 0)
    inside = jnp.where(row < OWN, (me > 0).astype(F32), (me < groups - 1).astype(F32))
    upper_sides[...] = (dot(bins, upper[0]) + dot(bins, upper[1])) * inside
    settle(out_second, in_second, send_second, recv_second)

    packed[pl.ds(0, PACK * groups), :] = in_second[...].astype(F32).reshape(PACK * groups, OWN)

    def turn(*firsts):
        parts = [[packed[pl.ds(first + part, groups, stride=PACK), :] for first in firsts] for part in range(4)]
        return jnp.concatenate([sum(part[1:], part[0]).T for part in parts], axis=1)

    back_high, back_low = split(turn(0, 4))
    all_bins = jnp.concatenate([back_high, back_low, turn(8).astype(BF16), turn(12).astype(BF16)], axis=0)
    chunk = 256
    for number in range(LENGTH // chunk):
        span = pl.ds(number * chunk, chunk)
        sums = dot(all_bins, time_high[:, span])
        rejected = (sums[:OWN] + sums[OWN:2 * OWN]) + dot(back_high, time_low[:, span])
        ext[pl.ds(OWN, OWN), span] = (signal[:, span] + rejected).astype(BF16)
        ext[pl.ds(0, OWN), span] = (upper_sides[pl.ds(0, OWN), span] + sums[2 * OWN:3 * OWN]).astype(BF16)
        ext[pl.ds(2 * OWN, OWN), span] = (upper_sides[pl.ds(OWN, OWN), span] + sums[3 * OWN:]).astype(BF16)
    own = ext[pl.ds(OWN, OWN), :] * jnp.asarray(1.0 / math.sqrt(LENGTH), BF16)
    half = OWN // 2
    for lag in range(LAGS):
        shifted = own if lag == 0 else jnp.concatenate(
            [jnp.zeros((OWN, lag), BF16), own[:, :LENGTH - lag]], axis=1
        )
        lags[0, pl.ds(lag * half, half), :] = shifted[:half]
        lags[1, pl.ds((lag ^ 1) * half, half), :] = shifted[half:]

    span = 3 * OWN - half
    front = lax.broadcasted_iota(jnp.int32, (span - half, OWN), 1) < half
    for number in range(LAGS // 4):
        rows = pl.ds(number * 4 * half, 4 * half)
        first = dot(ext[pl.ds(0, span), :], lags[0, rows, :], ((1,), (1,)))
        second = dot(ext[pl.ds(half, span), :], lags[1, rows, :], ((1,), (1,)))
        for lag in range(4):
            lanes = slice(lag // 2 * OWN, (lag // 2 + 1) * OWN)
            begin = 4 * number + lag
            low, high = first[:, lanes], second[:, lanes]
            both = (low[half:], high[:span - half])
            lagged[pl.ds(begin, half, stride=LAGS), :] = low[:half]
            lagged[pl.ds(half * LAGS + begin, span - half, stride=LAGS), :] = jnp.where(front, both[lag % 2], both[1 - lag % 2])
            lagged[pl.ds(span * LAGS + begin, half, stride=LAGS), :] = high[span - half:]
    for copy in early:
        copy.wait_send()


def write_kernel(lagged, out_far, out, store_sem):
    done = 0
    for last in range(TILE_ROWS + TILES // 4 - 1, TILE_ROWS + TILES, TILES // 4):
        finish(lagged, out, done, last)
        done = last
        columns = pl.ds((last - TILE_ROWS + 1 - TILES // 4) * OWN, TILES // 4 * OWN)
        pltpu.make_async_copy(out.at[:, columns], out_far.at[:, columns], store_sem).start()
    pltpu.make_async_copy(out, out_far, store_sem).wait()


def body(groups, inner, signal, fan_cut):
    operands = [signal, fan_cut.reshape(OWN, groups), *(jnp.asarray(table) for table in tables(groups))]
    operands = [pltpu.with_memory_space_constraint(array, pltpu.HBM) for array in operands]
    far = pl.BlockSpec(memory_space=pltpu.HBM)
    messages = [pltpu.VMEM((groups, 4, OWN), F32)] * 2 + [pltpu.VMEM((groups, PACK, OWN), BF16)] * 2
    lagged = pl.pallas_call(
        functools.partial(filter_kernel, groups, inner),
        out_shape=pltpu.VMEM(((3 * OWN + 1) * LAGS, OWN), F32),
        in_specs=[far] * len(operands),
        out_specs=pl.BlockSpec(memory_space=pltpu.VMEM),
        scratch_shapes=[pltpu.VMEM(array.shape, array.dtype) for array in operands]
        + [pltpu.SemaphoreType.DMA((len(operands) + 1,))]
        + messages + [pltpu.SemaphoreType.DMA] * 4 + [pltpu.SemaphoreType.DMA((2,))] * 2
        + [
            pltpu.VMEM((OWN, 2 * BINS), BF16),
            pltpu.VMEM((2, OWN, 2 * BINS), BF16),
            pltpu.VMEM((2 * OWN, LENGTH), F32),
            pltpu.VMEM((PACK * (groups + 4), OWN), F32),
            pltpu.VMEM((3 * OWN, LENGTH), BF16),
            pltpu.VMEM((2, LAGS * OWN // 2, LENGTH), BF16),
        ],
        compiler_params=pltpu.CompilerParams(
            collective_id=0, has_side_effects=True, vmem_limit_bytes=40 * 2**20
        ),
        name="fan_filter_products",
    )(*operands)
    lagged = pltpu.with_memory_space_constraint(lagged, pltpu.VMEM)
    return pl.pallas_call(
        write_kernel,
        out_shape=jax.ShapeDtypeStruct((OWN, BAND * LAGS), F32),
        in_specs=[pl.BlockSpec(memory_space=pltpu.VMEM)],
        out_specs=far,
        scratch_shapes=[pltpu.VMEM((OWN, BAND * LAGS), F32), pltpu.SemaphoreType.DMA],
        compiler_params=pltpu.CompilerParams(vmem_limit_bytes=20 * 2**20),
        name="correlation_rows",
    )(lagged)


def solution(mesh):
    groups, inner = mesh.size, mesh.shape["cy"]
    return jax.shard_map(
        functools.partial(body, groups, inner),
        mesh=mesh,
        in_specs=(P(("cx", "cy"), None), P()),
        out_specs=P(("cx", "cy"), None),
        check_vma=False,
    )
```

```python
import functools
import itertools
import math

import jax
import jax.numpy as jnp
import numpy as np
from jax import lax
from jax.experimental import pallas as pl
from jax.experimental.pallas import tpu as pltpu
from jax.sharding import PartitionSpec as P

BAND = 256
LAGS = 16
BINS = 256
OWN = 128
LENGTH = 1024
MESH = pl.DeviceIdType.MESH
F32 = jnp.float32
BF16 = jnp.bfloat16


def halves(table):
    high = table.astype(BF16)
    return high, (table - high.astype(np.float64)).astype(BF16)


def tables(groups):
    bin_index = np.arange(BINS, dtype=np.int64)
    angle = 2.0 * math.pi / LENGTH * (bin_index[:, None] * np.arange(LENGTH)[None, :] % LENGTH)
    pairs = np.stack([np.cos(angle), -np.sin(angle)], axis=1).reshape(groups, 2, 2, LENGTH)
    time = pairs.transpose(2, 1, 0, 3).reshape(2 * BINS, LENGTH)
    time[2 * groups] = np.cos(math.pi * np.arange(LENGTH))
    angle = 2.0 * math.pi / LENGTH * ((bin_index + BINS)[:, None] * np.arange(LENGTH)[None, :] % LENGTH)
    upper = np.concatenate([np.cos(angle), -np.sin(angle)])
    index = np.arange(groups)
    angle = 2.0 * math.pi / groups * (index[:, None] * index[None, :] % groups)
    re, im = np.cos(angle), -np.sin(angle)
    wide = np.block([[re, -im], [im, re]])
    angle = 2.0 * math.pi / (groups * OWN) * (index[:, None] * index[None, :])
    twist = np.stack([np.cos(angle), np.sin(angle)]).astype(np.float32)
    return np.stack(halves(time)), np.stack([*halves(wide), *halves(wide.T)]), twist, np.stack(halves(upper))


def dot(left, right, dims=((1,), (0,))):
    return lax.dot_general(left, right, (dims, ((), ())), preferred_element_type=F32)


def split(value):
    high = value.astype(BF16)
    return high, (value - high.astype(F32)).astype(BF16)


def dot_three(left, right):
    return dot(left[0], right[0]) + (dot(left[0], right[1]) + dot(left[1], right[0]))


def least_cut(cut):
    row = lax.broadcasted_iota(jnp.int32, (OWN, OWN), 0)
    col = lax.broadcasted_iota(jnp.int32, (OWN, OWN), 1)
    mirror = (((row + col) % OWN) == 0).astype(F32).astype(BF16)
    reverse = ((row + col) == OWN - 1).astype(F32).astype(BF16)
    exact = cut.astype(F32).astype(BF16)
    across = dot(exact, mirror).astype(BF16)
    mirrored = jnp.where(col == 0, dot(mirror, across), dot(reverse, across))
    return jnp.maximum(cut.astype(F32), mirrored).T


TILES = BAND * LAGS // OWN
TILE_ROWS = OWN // 8
PACK = 16


def finish(lagged, out, first, last):
    lane = lax.broadcasted_iota(jnp.int32, (8, OWN), 1)
    odd = [(lane // step) % 2 == 1 for step in (1, 2, 4)]
    known = {}

    def skewed(bit, spot):
        if (bit, spot) not in known:
            known[bit, spot] = lagged[pl.ds(8 * spot, 8), :] if bit == 0 else jnp.where(
                odd[bit - 1], skewed(bit - 1, spot + (1 << bit)), skewed(bit - 1, spot)
            )
        return known[bit, spot]

    for tile in range(first, last):
        turned = jnp.concatenate([skewed(3, tile * TILE_ROWS + number) for number in range(TILE_ROWS)], axis=0).T
        for group in range(max(0, tile - TILES + 1), min(TILE_ROWS, tile + 1)):
            out[pl.ds(8 * group, 8), pl.ds((tile - group) * OWN, OWN)] = turned[8 * group:8 * group + 8]


def filter_kernel(
    groups, inner,
    signal_far, cut_far, time_far, wide_far, twist_far, upper_far,
    lagged,
    signal, cut, time, wide_all, twist, upper, load_sems,
    out_first, in_first, out_second, in_second,
    send_first, recv_first, send_second, recv_second, send_upper, recv_upper,
    upper_out, upper_in, upper_sides, packed, ext, lags,
):
    outer_at, inner_at = lax.axis_index("cx"), lax.axis_index("cy")
    me = outer_at * inner + inner_at

    def at(device):
        return (device // inner, device % inner)

    def peer(step):
        return lax.rem(me + step, groups)

    def visit_others(visit):
        high, mid, core = outer_at // 8, lax.rem(outer_at // 2, 4), lax.rem(outer_at, 2)
        top, low = inner_at // 4, lax.rem(inner_at, 4)
        highs, cores, tops = (8 * high, 8 - 8 * high), (core, 1 - core), (4 * top, 4 - 4 * top)
        mids = [2 * lax.rem(mid + step, 4) for step in range(4)]
        lows = [lax.rem(low + step, 4) for step in range(4)]
        ring = (0, 1, 2, 1)
        offsets = sorted(
            itertools.product(range(4), range(4), range(2), range(2), range(2)),
            key=lambda o: (-(ring[o[0]] + ring[o[1]] + 2 * o[2] + o[3]),
                           (o[0] * 7 + o[1] * 5 + o[2] * 3 + o[3] * 11 + o[4] * 13) % 17),
        )
        for mid_step, low_step, flip_top, flip_high, flip_core in offsets:
            if mid_step + low_step + flip_top + flip_high + flip_core > 0:
                visit(highs[flip_high] + mids[mid_step] + cores[flip_core], tops[flip_top] + lows[low_step])

    pairs = ((signal_far, signal), (time_far.at[0], time.at[0]), (time_far.at[1], time.at[1]),
             (cut_far, cut), (wide_far, wide_all), (twist_far, twist), (upper_far, upper))
    loads = [pltpu.make_async_copy(far, near, load_sems.at[number]) for number, (far, near) in enumerate(pairs)]
    for load in loads[:-1]:
        load.start()

    barrier = pltpu.get_barrier_semaphore()

    def greet(cx, cy):
        pl.semaphore_signal(barrier, inc=1, device_id=(cx, cy), device_id_type=MESH)

    visit_others(greet)
    loads[0].wait()
    time_high, time_low = time.at[0], time.at[1]
    own_high, own_low = split(signal[...])
    both = jnp.concatenate([own_high, own_low], axis=0)
    loads[1].wait()
    wide_sum = dot(time_high[...], both, ((1,), (1,)))
    loads[2].wait()
    spectrum = (wide_sum[:, :OWN] + wide_sum[:, OWN:]) + dot(time_low[...], own_high, ((1,), (1,)))
    for part in range(4):
        out_first[:, part, :] = spectrum[part * OWN:(part + 1) * OWN]

    loads[-1].start()
    pl.semaphore_wait(barrier, groups - 1)

    def exchange(outgoing, incoming, send_sem, recv_sem):
        def push(cx, cy):
            pltpu.make_async_remote_copy(
                src_ref=outgoing.at[cx * inner + cy],
                dst_ref=incoming.at[me],
                send_sem=send_sem,
                recv_sem=recv_sem,
                device_id=(cx, cy),
                device_id_type=MESH,
            ).start()

        visit_others(push)
        incoming[me] = outgoing[me]

    def settle(outgoing, incoming, send_sem, recv_sem):
        rest = pltpu.make_async_remote_copy(
            src_ref=outgoing.at[pl.ds(0, groups - 1)],
            dst_ref=incoming.at[pl.ds(0, groups - 1)],
            send_sem=send_sem,
            recv_sem=recv_sem,
            device_id=at(peer(1)),
            device_id_type=MESH,
        )
        rest.wait_recv()
        return rest

    exchange(out_first, in_first, send_first, recv_first)
    for load in loads[3:]:
        load.wait()
    upper_sum = dot(both, upper[0], ((1,), (1,)))
    upper_sum = (upper_sum[:OWN] + upper_sum[OWN:]) + dot(own_high, upper[1], ((1,), (1,)))
    upper_out[...] = (upper_sum * (2.0 / LENGTH)).astype(BF16)

    early = [
        pltpu.make_async_remote_copy(
            src_ref=upper_out, dst_ref=upper_in.at[side],
            send_sem=send_upper.at[side], recv_sem=recv_upper.at[side],
            device_id=at(peer(1 if side == 0 else groups - 1)), device_id_type=MESH,
        )
        for side in range(2)
    ]
    for copy in early:
        copy.start()
    cut_least = least_cut(cut[...])
    wide = (wide_all[0], wide_all[1])
    flip = (wide_all[2], wide_all[3])
    cosine, sine = twist[0], twist[1]
    sent_first = settle(out_first, in_first, send_first, recv_first)

    rows = [in_first[:, part, :] for part in range(4)]
    real_zero = rows[2] * jnp.where(me == 0, 0.0, 1.0)
    values = [jnp.concatenate(pair, axis=0) for pair in ((rows[0], real_zero), (rows[1], rows[3]))]
    values = [dot_three(wide, split(value)) for value in values]
    values = [
        jnp.concatenate([re * cosine + im * sine, im * cosine - re * sine], axis=1)
        for re, im in ((value[:OWN], value[OWN:]) for value in values)
    ]
    values = [dot_three(split(value), flip) for value in values]
    even = (2 * me).astype(F32)
    scale = -2.0 / (LENGTH * groups * OWN)
    rejects = (
        jnp.where(cut_least > even, jnp.where(me == 0, 0.5 * scale, scale), 0.0),
        jnp.where(cut_least > even + 1.0, scale, 0.0),
    )
    values = [value * jnp.concatenate([reject, reject], axis=1) for value, reject in zip(values, rejects)]
    values = [dot_three(split(value), wide) for value in values]
    values = [
        jnp.concatenate([re * cosine - im * sine, im * cosine + re * sine], axis=0)
        for re, im in ((value[:, :OWN], value[:, OWN:]) for value in values)
    ]
    values = [dot_three(flip, split(value)) for value in values]
    for part in range(4):
        block = values[part % 2][(part // 2) * OWN:(part // 2 + 1) * OWN]
        weight = 2.0 / LENGTH if part % 2 else jnp.where(me == 0, 1.0 / LENGTH, 2.0 / LENGTH)
        kept = rows[part] * weight + block
        for first, array in (
            (PACK, block), (PACK + 4, block - block.astype(BF16).astype(F32)), (2 * PACK + 8, kept), (12, kept),
        ):
            packed[pl.ds(first + part, groups, stride=PACK), :] = array
    for first in (PACK + 8, PACK * groups + 12):
        packed[pl.ds(first, 4), :] = jnp.zeros((4, OWN), F32)
    out_second[...] = packed[pl.ds(PACK, PACK * groups), :].astype(BF16).reshape(groups, PACK, OWN)

    exchange(out_second, in_second, send_second, recv_second)
    for copy in early:
        copy.wait_recv()
    bins = upper_in[...].reshape(2 * OWN, 2 * BINS)
    row = lax.broadcasted_iota(jnp.int32, (2 * OWN, LENGTH), 0)
    inside = jnp.where(row < OWN, (me > 0).astype(F32), (me < groups - 1).astype(F32))
    upper_sides[...] = (dot(bins, upper[0]) + dot(bins, upper[1])) * inside
    sent_second = settle(out_second, in_second, send_second, recv_second)

    packed[pl.ds(0, PACK * groups), :] = in_second[...].astype(F32).reshape(PACK * groups, OWN)

    def turn(*firsts):
        parts = [[packed[pl.ds(first + part, groups, stride=PACK), :] for first in firsts] for part in range(4)]
        return jnp.concatenate([sum(part[1:], part[0]).T for part in parts], axis=1)

    back_high, back_low = split(turn(0, 4))
    all_bins = jnp.concatenate([back_high, back_low, turn(8).astype(BF16), turn(12).astype(BF16)], axis=0)
    chunk = 256
    for number in range(LENGTH // chunk):
        span = pl.ds(number * chunk, chunk)
        sums = dot(all_bins, time_high[:, span])
        rejected = (sums[:OWN] + sums[OWN:2 * OWN]) + dot(back_high, time_low[:, span])
        ext[pl.ds(OWN, OWN), span] = (signal[:, span] + rejected).astype(BF16)
        ext[pl.ds(0, OWN), span] = (upper_sides[pl.ds(0, OWN), span] + sums[2 * OWN:3 * OWN]).astype(BF16)
        ext[pl.ds(2 * OWN, OWN), span] = (upper_sides[pl.ds(OWN, OWN), span] + sums[3 * OWN:]).astype(BF16)
    own = ext[pl.ds(OWN, OWN), :] * jnp.asarray(1.0 / math.sqrt(LENGTH), BF16)
    for lag in range(LAGS):
        lags[pl.ds(lag * OWN, OWN), :] = own if lag == 0 else jnp.concatenate(
            [jnp.zeros((OWN, lag), BF16), own[:, :LENGTH - lag]], axis=1
        )

    everything = ext[...]
    for number in range(LAGS // 2):
        values = dot(everything, lags[pl.ds(number * 2 * OWN, 2 * OWN), :], ((1,), (1,)))
        for side in range(2):
            lagged[pl.ds(2 * number + side, 3 * OWN, stride=LAGS), :] = values[:, side * OWN:(side + 1) * OWN]
    for copy in (sent_first, sent_second, *early):
        copy.wait_send()


def write_kernel(lagged, out_far, out, store_sem):
    done = 0
    for last in range(TILE_ROWS + TILES // 4 - 1, TILE_ROWS + TILES, TILES // 4):
        finish(lagged, out, done, last)
        done = last
        columns = pl.ds((last - TILE_ROWS + 1 - TILES // 4) * OWN, TILES // 4 * OWN)
        pltpu.make_async_copy(out.at[:, columns], out_far.at[:, columns], store_sem).start()
    pltpu.make_async_copy(out, out_far, store_sem).wait()


def body(groups, inner, signal, fan_cut):
    operands = [signal, fan_cut.reshape(OWN, groups), *(jnp.asarray(table) for table in tables(groups))]
    operands = [pltpu.with_memory_space_constraint(array, pltpu.HBM) for array in operands]
    far = pl.BlockSpec(memory_space=pltpu.HBM)
    messages = [pltpu.VMEM((groups, 4, OWN), F32)] * 2 + [pltpu.VMEM((groups, PACK, OWN), BF16)] * 2
    lagged = pl.pallas_call(
        functools.partial(filter_kernel, groups, inner),
        out_shape=pltpu.VMEM(((3 * OWN + 1) * LAGS, OWN), F32),
        in_specs=[far] * len(operands),
        out_specs=pl.BlockSpec(memory_space=pltpu.VMEM),
        scratch_shapes=[pltpu.VMEM(array.shape, array.dtype) for array in operands]
        + [pltpu.SemaphoreType.DMA((len(operands) + 1,))]
        + messages + [pltpu.SemaphoreType.DMA] * 4 + [pltpu.SemaphoreType.DMA((2,))] * 2
        + [
            pltpu.VMEM((OWN, 2 * BINS), BF16),
            pltpu.VMEM((2, OWN, 2 * BINS), BF16),
            pltpu.VMEM((2 * OWN, LENGTH), F32),
            pltpu.VMEM((PACK * (groups + 4), OWN), F32),
            pltpu.VMEM((3 * OWN, LENGTH), BF16),
            pltpu.VMEM((LAGS * OWN, LENGTH), BF16),
        ],
        compiler_params=pltpu.CompilerParams(
            collective_id=0, has_side_effects=True, vmem_limit_bytes=40 * 2**20
        ),
        name="fan_filter_products",
    )(*operands)
    lagged = pltpu.with_memory_space_constraint(lagged, pltpu.VMEM)
    return pl.pallas_call(
        write_kernel,
        out_shape=jax.ShapeDtypeStruct((OWN, BAND * LAGS), F32),
        in_specs=[pl.BlockSpec(memory_space=pltpu.VMEM)],
        out_specs=far,
        scratch_shapes=[pltpu.VMEM((OWN, BAND * LAGS), F32), pltpu.SemaphoreType.DMA],
        compiler_params=pltpu.CompilerParams(vmem_limit_bytes=20 * 2**20),
        name="correlation_rows",
    )(lagged)


def solution(mesh):
    groups, inner = mesh.size, mesh.shape["cy"]
    return jax.shard_map(
        functools.partial(body, groups, inner),
        mesh=mesh,
        in_specs=(P(("cx", "cy"), None), P()),
        out_specs=P(("cx", "cy"), None),
        check_vma=False,
    )
```
